512 devices in a mesh: tile: 128 (over y, z, core), dp: 4 (over x).
Axes of the slice: x: 4, y: 8, z: 8, core: 2. Of those that a mesh axis runs over, the one named last changes fastest.
Arguments:
- features: bfloat16 [4, 1024, 128, 128], P('dp', 'tile'), may hold values from -6 to 6
- w_sub: bfloat16 [27, 128, 128], replicated, may hold values from -0.109375 to 0.109375
- w_down: bfloat16 [8, 128, 256], replicated, may hold values from -0.1875 to 0.1875
- cotangent: bfloat16 [4, 512, 128, 256], P('dp', 'tile'), may hold values from -6 to 6
- vox_mask: int32 [4, 1024, 128], P('dp', 'tile'), may hold values from 0 to 1, as said below
- nbr_owner: int32 [4, 1024, 27], P('dp', 'tile'), may hold values from -1 to 127, as said below
- nbr_slot: int32 [4, 1024, 27], P('dp', 'tile'), may hold values from 0 to 7, as said below
- voxel_map: int32 [4, 1024, 27, 128], P('dp', 'tile'), may hold values from -1 to 127, as said below
- parent_slot: int32 [4, 1024], P('dp', 'tile'), may hold values from 0 to 3, as said below
- parent_octant: int32 [4, 1024], P('dp', 'tile'), may hold values from 0 to 7, as said below
Outputs:
- coarse_out: bfloat16 [4, 512, 128, 256], P('dp', 'tile')
- grad_input: bfloat16 [4, 1024, 128, 128], P('dp', 'tile')
- grad_sub_flat: float32 [442368], P('tile')
- grad_down_flat: float32 [262144], P('tile')
The draws below stay inside these ranges and needn't reach their ends.
Inputs may be any that keep to these rules, and one draw needn't show every extreme that they name: `vox_mask`: in each tile the slots that hold only zeros lie just before its last 2 slots. `nbr_owner`: A neighbour lies on the block's own tile, on the tile before it (then in one of that tile's last 2 slots, and only for the first 2 blocks of a tile) or on the tile after it (then in one of its first 2 slots, and only for the last 2 blocks of a tile). Offset 13 is the block itself. `nbr_slot`: 0 where there is no neighbour. `voxel_map`: at offset 13 every voxel reads itself. `parent_slot`: each coarse block of a tile receives exactly two fine blocks of that tile. `parent_octant`: the two fine blocks of one coarse block have different octants.
All inputs are finite; a program needn't handle non-finite values.
Results may differ from the reference program's by a relative error of at most 0.007.
Values may be sent and summed in bfloat16 or wider, within the bound.
A program may use at most 64 MiB of HBM per device.

```python
import jax
import jax.numpy as jnp
import numpy as np
from jax import lax

BLK_DEV = 8
FACE = 2
C = 128
C2 = 256
BV = 128
SCENES = 4
BLOCKS = 1024
CBLK_DEV = 4
CBLOCKS = 512


def neighbours(key):
    base_key = jax.random.fold_in(key, 202)
    key_one, key_two, key_three = jax.random.split(base_key, 3)
    tile_count = BLOCKS // BLK_DEV
    grid_shape = (SCENES, tile_count, BLK_DEV, 27)
    tile_ids = jnp.broadcast_to(jnp.arange(tile_count, dtype=jnp.int32)[None, :, None, None], grid_shape)
    slot_ids = jnp.broadcast_to(jnp.arange(BLK_DEV, dtype=jnp.int32)[None, None, :, None], grid_shape)
    offsets = jnp.broadcast_to(jnp.arange(27, dtype=jnp.int32)[None, None, None, :], grid_shape)
    choose = jax.random.randint(key_one, grid_shape, 0, 4)
    own_pick = jax.random.randint(key_two, grid_shape, 0, BLK_DEV)
    face_pick = jax.random.randint(key_three, grid_shape, 0, FACE)
    owner_tile = jnp.where(choose == 1, -1, tile_ids)
    slot_index = own_pick
    go_below = (slot_ids < FACE) & (choose == 0)
    go_above = (slot_ids >= BLK_DEV - FACE) & (choose == 0)
    owner_tile = jnp.where(go_below, tile_ids - 1, owner_tile)
    slot_index = jnp.where(go_below, BLK_DEV - FACE + face_pick, slot_index)
    owner_tile = jnp.where(go_above, tile_ids + 1, owner_tile)
    slot_index = jnp.where(go_above, face_pick, slot_index)
    owner_tile = jnp.where(owner_tile >= tile_count, -1, owner_tile)
    owner_tile = jnp.where(offsets == 13, tile_ids, owner_tile)
    slot_index = jnp.where(offsets == 13, slot_ids, slot_index)
    slot_index = jnp.where(owner_tile < 0, 0, slot_index)
    return (owner_tile.reshape(SCENES, BLOCKS, 27), slot_index.reshape(SCENES, BLOCKS, 27))


def parents(key):
    base_key = jax.random.fold_in(key, 404)
    key_one, key_two, key_three = jax.random.split(base_key, 3)
    groups = SCENES * (BLOCKS // BLK_DEV)
    scores = jax.random.randint(key_one, (groups, CBLK_DEV), 0, 1 << 20) * CBLK_DEV + jnp.arange(CBLK_DEV, dtype=jnp.int32)[None, :]
    coarse_order = jnp.argsort(scores, axis=1).astype(jnp.int32)
    first_octant = jax.random.randint(key_two, (groups, CBLK_DEV), 0, 8)
    octant_step = jax.random.randint(key_three, (groups, CBLK_DEV), 1, 8)
    second_octant = (first_octant + octant_step) % 8
    slot_ids = jnp.arange(BLK_DEV, dtype=jnp.int32)
    coarse_of = coarse_order[:, slot_ids % CBLK_DEV]
    octant_of = jnp.where(slot_ids[None, :] < CBLK_DEV, jnp.take_along_axis(first_octant, coarse_of, axis=1), jnp.take_along_axis(second_octant, coarse_of, axis=1))
    return (coarse_of.reshape(SCENES, BLOCKS), octant_of.reshape(SCENES, BLOCKS))


def draw_vox_mask(key, part):
    key = jax.random.fold_in(key, 3)
    key_one, key_two = jax.random.split(key)
    tile_count = BLOCKS // BLK_DEV
    padding = jax.random.randint(key_one, (SCENES, tile_count, 1), 0, BLK_DEV - 2 * FACE + 1)
    slot_ids = jnp.arange(BLK_DEV, dtype=jnp.int32)[None, None, :]
    padded = (slot_ids >= BLK_DEV - FACE - padding) & (slot_ids < BLK_DEV - FACE)
    present = (jax.random.randint(key_two, (SCENES, tile_count, BLK_DEV, BV), 0, 10) < 7).astype(jnp.int32)
    return jnp.where(padded[:, :, :, None], 0, present).reshape(SCENES, BLOCKS, BV)


def draw_nbr_owner(key, part):
    owner_tile, slot_index = neighbours(key)
    return owner_tile


def draw_nbr_slot(key, part):
    owner_tile, slot_index = neighbours(key)
    return slot_index


def draw_voxel_map(key, part):
    key = jax.random.fold_in(key, 5)
    key_one, key_two = jax.random.split(key)
    grid_shape = (SCENES, BLOCKS, 27, BV)
    missing = jax.random.randint(key_one, grid_shape, 0, 4) == 0
    picked_voxel = jax.random.randint(key_two, grid_shape, 0, BV)
    offsets = jnp.arange(27, dtype=jnp.int32)[None, None, :, None]
    itself = jnp.broadcast_to(jnp.arange(BV, dtype=jnp.int32)[None, None, None, :], grid_shape)
    result = jnp.where(missing, -1, picked_voxel)
    return jnp.where(offsets == 13, itself, result)


def draw_parent_slot(key, part):
    coarse_of, octant_of = parents(key)
    return coarse_of


def draw_parent_octant(key, part):
    coarse_of, octant_of = parents(key)
    return octant_of


def levels(rng, dims, shards, low, top_value):
    def one(dim, blocks):
        heights = jax.random.uniform(jax.random.fold_in(jax.random.fold_in(rng, 6), dim), (blocks,), jnp.float32, low / len(shards), top_value / len(shards))
        return jnp.repeat(jnp.exp(heights), dims[dim] // blocks).reshape((-1,) + (1,) * (len(dims) - dim - 1))

    factor_of = one(*shards[0])
    for cut in shards[1:]:
        factor_of = factor_of * one(*cut)
    return factor_of


def normal_values(rng, shape, scale, limit, cuts=(), kind=jnp.bfloat16):
    drawn = scale * jax.random.normal(rng, shape, jnp.float32)
    if cuts:
        drawn = drawn * levels(rng, shape, cuts, -0.22, 0.18)
    return jnp.clip(drawn, -limit, limit).astype(kind)


def setup_inputs(seed: int = 0) -> dict:
    seeds = jax.random.split(jax.random.key(seed), 11)
    features = normal_values(seeds[0], (SCENES, BLOCKS, BV, C), 1.0, 6.0, ((0, 4), (1, 128)))
    w_sub = normal_values(seeds[1], (27, C, C), (27 * C) ** -0.5, 0.109375)
    w_down = normal_values(seeds[2], (8, C, C2), (8 * C) ** -0.5, 0.1875)
    cotangent = normal_values(seeds[3], (SCENES, CBLOCKS, BV, C2), 1.0, 6.0, ((0, 4), (1, 128)))
    vox_mask = draw_vox_mask(jax.random.fold_in(seeds[10], 71), 0)
    nbr_owner = draw_nbr_owner(jax.random.fold_in(seeds[10], 71), 0)
    nbr_slot = draw_nbr_slot(jax.random.fold_in(seeds[10], 71), 0)
    voxel_map = draw_voxel_map(jax.random.fold_in(seeds[10], 71), 0)
    parent_slot = draw_parent_slot(jax.random.fold_in(seeds[10], 71), 0)
    parent_octant = draw_parent_octant(jax.random.fold_in(seeds[10], 71), 0)
    return {"features": features, "w_sub": w_sub, "w_down": w_down, "cotangent": cotangent, "vox_mask": vox_mask, "nbr_owner": nbr_owner, "nbr_slot": nbr_slot, "voxel_map": voxel_map, "parent_slot": parent_slot, "parent_octant": parent_octant}


def octant_table(block_depth):
    half_depth = block_depth // 2
    octants = np.arange(8)
    places = np.arange(4 * half_depth)
    big_z = (octants // 4)[:, None] * half_depth + (places // 4)[None, :]
    big_y = ((octants // 2) % 2)[:, None] * 2 + ((places // 2) % 2)[None, :]
    big_x = (octants % 2)[:, None] * 2 + (places % 2)[None, :]
    return (big_z * 16 + big_y * 4 + big_x).astype(np.int32)


def coarse_rows(coarse_block, octant_ids, block_depth):
    octant_rows = jnp.asarray(octant_table(block_depth))
    matches = (octant_ids[:, None] == jnp.arange(8, dtype=jnp.int32)[None, :]).astype(jnp.int32)
    within = jnp.sum(matches[:, :, None] * octant_rows[None, :, :], axis=1)
    return coarse_block[:, None] * (16 * block_depth) + within


def to_children(fine_blocks):
    count, voxels, channels = fine_blocks.shape
    half_depth = voxels // 32
    shaped = fine_blocks.reshape(count, half_depth, 2, 2, 2, 2, 2, channels)
    shaped = jnp.transpose(shaped, (0, 2, 4, 6, 1, 3, 5, 7))
    return shaped.reshape(count, 8, voxels // 8, channels)


def from_children(child_blocks):
    count, eight, places, channels = child_blocks.shape
    half_depth = places // 4
    shaped = child_blocks.reshape(count, 2, 2, 2, half_depth, 2, 2, channels)
    shaped = jnp.transpose(shaped, (0, 4, 1, 5, 2, 6, 3, 7))
    return shaped.reshape(count, places * 8, channels)


def reference(features, w_sub, w_down, cotangent, vox_mask, nbr_owner, nbr_slot, voxel_map, parent_slot, parent_octant):
    channels = features.shape[3]
    out_width = w_down.shape[2]
    grad_sub = jnp.zeros(w_sub.shape, jnp.float32)
    grad_down = jnp.zeros(w_down.shape, jnp.float32)
    coarse_list = []
    input_list = []
    for scene in range(SCENES):
        active = vox_mask[scene] > 0
        keep_f = active.reshape(-1, 1).astype(jnp.float32)
        masked = jnp.where(active[:, :, None], features[scene], jnp.zeros((), features.dtype))
        flat_rows = masked.reshape(-1, channels)
        position = nbr_owner[scene] * BLK_DEV + nbr_slot[scene]
        usable = (nbr_owner[scene] >= 0)[:, :, None] & (voxel_map[scene] >= 0)
        source_rows = jnp.where(usable, position[:, :, None] * BV + voxel_map[scene], 0).astype(jnp.int32)
        source_rows = jnp.transpose(source_rows, (1, 0, 2)).reshape(27, -1)
        usable = jnp.transpose(usable, (1, 0, 2)).reshape(27, -1)

        def gathered(row_k, valid_k):
            return jnp.where(valid_k[:, None], flat_rows[row_k], jnp.zeros((), flat_rows.dtype))

        def forward_step(running, element):
            row_k, valid_k, weight_k = element
            return running + jnp.dot(gathered(row_k, valid_k), weight_k, preferred_element_type=jnp.float32), None

        pre_act, _ = lax.scan(forward_step, jnp.zeros((flat_rows.shape[0], channels), jnp.float32), (source_rows, usable, w_sub))
        hidden = (keep_f * jax.nn.silu(pre_act)).astype(jnp.bfloat16)
        children = to_children(hidden.reshape(BLOCKS, BV, channels))
        coarse_block = (jnp.arange(BLOCKS, dtype=jnp.int32) // BLK_DEV) * CBLK_DEV + parent_slot[scene]
        coarse_row = coarse_rows(coarse_block, parent_octant[scene], BV // 16)
        partial_value = jnp.einsum('ncuk,ckj->nuj', children.astype(jnp.float32), w_down.astype(jnp.float32))
        coarse = jnp.zeros((CBLOCKS * BV, out_width), jnp.float32).at[coarse_row.reshape(-1)].add(partial_value.reshape(-1, out_width))
        coarse_list.append(coarse.astype(jnp.bfloat16).reshape(CBLOCKS, BV, out_width))
        picked = cotangent[scene].reshape(-1, out_width)[coarse_row]
        dchildren = jnp.einsum('nuj,ckj->ncuk', picked.astype(jnp.float32), w_down.astype(jnp.float32))
        grad_down = grad_down + jnp.einsum('ncuk,nuj->ckj', children.astype(jnp.float32), picked.astype(jnp.float32))
        dhidden = from_children(dchildren).reshape(-1, channels)
        sigmoid_pre = jax.nn.sigmoid(pre_act)
        dpre = (keep_f * dhidden * sigmoid_pre * (1.0 + pre_act * (1.0 - sigmoid_pre))).astype(jnp.bfloat16)

        def backward_step(running, element):
            row_k, valid_k, weight_k = element
            gathered_k = gathered(row_k, valid_k)
            grad_k = jnp.dot(gathered_k.T, dpre, preferred_element_type=jnp.float32)
            term_k = lax.dot_general(dpre, weight_k, (((1,), (1,)), ((), ())), preferred_element_type=jnp.float32)
            running = running.at[row_k].add(jnp.where(valid_k[:, None], term_k, jnp.zeros((), jnp.float32)))
            return running, grad_k

        grad_rows, per_offset = lax.scan(backward_step, jnp.zeros((flat_rows.shape[0], channels), jnp.float32), (source_rows, usable, w_sub))
        grad_sub = grad_sub + per_offset
        input_list.append((keep_f * grad_rows).astype(jnp.bfloat16).reshape(BLOCKS, BV, channels))
    grad_scale = float(SCENES * BLOCKS * BV) ** -0.5
    return (jnp.stack(coarse_list), jnp.stack(input_list), (grad_sub * grad_scale).reshape(-1), (grad_down * grad_scale).reshape(-1))
```

```python
import functools

import jax
import jax.numpy as jnp
from jax import lax
from jax.experimental import pallas as pl
from jax.experimental.pallas import tpu as pltpu
from jax.sharding import PartitionSpec as P

FACE = 2
MESH = pl.DeviceIdType.MESH


G = 2
SUB_W, DOWN_W, ROW_W, SLOT = 7, 4, 12, 16


def reduce_kernel(
    sizes, scale, parts_ref, out_ref, send0, recv0, acc1, send1, recv1, acc2, send2, recv2,
    zbuf, recv3, fin, gath, ss0, rs0, ss1, rs1, ss2, rs2, ss3, rs3, ss4, rs4,
):
    nx, ny, nz = sizes
    rows = parts_ref.shape[4]
    tile = lax.axis_index("tile")
    x = lax.axis_index("dp")
    core = lax.rem(tile, 2)
    z = lax.rem(tile // 2, nz)
    y = tile // (2 * nz)
    other = 1 - core
    f32, bf16 = jnp.float32, jnp.bfloat16

    def place(yy, zz, cc):
        return (yy * nz + zz) * 2 + cc

    x_peers = [lax.rem(x + d, nx) for d in range(1, nx)]
    y_peers = [lax.rem(y + d, ny) for d in range(1, ny)]
    z_peers = [lax.rem(z + d, nz) for d in range(1, nz)]
    group = [(f, d) for f in (0, 1) for d in range(nx) if (f, d) != (0, 0)]

    def worker(f, d):
        cc = core if f == 0 else other
        return cc, lax.rem(x + d, nx)

    barrier = pltpu.get_barrier_semaphore()
    for f, d in group:
        cc, xx = worker(f, d)
        pl.semaphore_signal(barrier, inc=1, device_id=(place(y, z, cc), xx), device_id_type=MESH)
    for yy in y_peers:
        pl.semaphore_signal(barrier, inc=1, device_id=(place(yy, z, core), x), device_id_type=MESH)
    for zz in z_peers:
        pl.semaphore_signal(barrier, inc=1, device_id=(place(y, zz, core), x), device_id_type=MESH)

    copies = []

    def send(src, dst, ss, rs, t, xx):
        copy = pltpu.make_async_remote_copy(
            src_ref=src, dst_ref=dst, send_sem=ss, recv_sem=rs,
            device_id=(t, xx), device_id_type=MESH,
        )
        copy.start()
        copies.append(copy)
        return copy

    def cast_half(g):
        def body(i, c):
            send0[g, i] = parts_ref[other, g, i].astype(bf16)
            return c
        lax.fori_loop(0, nx, body, 0)

    cast_half(0)
    pl.semaphore_wait(barrier, len(group) + ny - 1 + nz - 1)
    step0 = []
    for g in range(G):
        if g:
            cast_half(g)
        step0.append(send(send0.at[g], recv0.at[g], ss0.at[g], rs0.at[g], place(y, z, other), x))

    step1 = []
    for g in range(G):
        step0[g].wait_recv()

        def body(i, c):
            total = parts_ref[core, g, i] + recv0[g, i].astype(f32)
            acc1[g, i] = total
            send1[g, i] = total.astype(bf16)
            return c

        lax.fori_loop(0, nx, body, 0)
        step1.append([
            send(send1.at[g, xx], recv1.at[d, g], ss1.at[d, g], rs1.at[d, g], tile, xx)
            for d, xx in enumerate(x_peers)
        ])

    step2 = []
    for g in range(G):
        for copy in step1[g]:
            copy.wait_recv()

        def body(i, c):
            total = acc1[g, x, i]
            for d in range(nx - 1):
                total = total + recv1[d, g, i].astype(f32)
            acc2[g, i] = total
            send2[g, i] = total.astype(bf16)
            return c

        lax.fori_loop(0, ny, body, 0)
        step2.append([
            send(send2.at[g, yy], recv2.at[d, g], ss2.at[d, g], rs2.at[d, g], place(yy, z, core), x)
            for d, yy in enumerate(y_peers)
        ])

    zbuf[...] = jnp.zeros_like(zbuf)
    for g in range(G):
        for copy in step2[g]:
            copy.wait_recv()
        total = acc2[g, y]
        for d in range(ny - 1):
            total = total + recv2[d, g].astype(f32)
        each = rows // ROW_W
        for j in range(each):
            zbuf[g * each + j, 0:ROW_W, :] = total[j * ROW_W:(j + 1) * ROW_W]
    step3 = [
        send(zbuf.at[zz], recv3.at[d], ss3.at[d], rs3.at[d], place(y, zz, core), x)
        for d, zz in enumerate(z_peers)
    ]
    for copy in step3:
        copy.wait_recv()
    total = zbuf[z]
    for d in range(nz - 1):
        total = total + recv3[d]
    total = total * scale
    fin[...] = total
    mine = core * nx + x
    step4 = []
    for i, (f, d) in enumerate(group):
        cc, xx = worker(f, d)
        step4.append(send(fin, gath.at[mine], ss4.at[i], rs4.at[i], place(y, z, cc), xx))
    gath[mine] = total
    for copy in step4:
        copy.wait_recv()
    out_ref[...] = gath[...]
    for copy in copies:
        copy.wait_send()


def reduce_parts(parts, sizes, scale):
    nx, ny, nz = sizes
    rows = parts.shape[4]
    f32, bf16 = jnp.float32, jnp.bfloat16
    dma = pltpu.SemaphoreType.DMA
    lanes = parts.shape[5]
    group = 2 * nx - 1
    return pl.pallas_call(
        functools.partial(reduce_kernel, sizes, scale),
        out_shape=jax.ShapeDtypeStruct((2 * nx, SLOT, lanes), f32),
        in_specs=[pl.BlockSpec(memory_space=pltpu.VMEM)],
        out_specs=pl.BlockSpec(memory_space=pltpu.VMEM),
        scratch_shapes=[
            pltpu.VMEM((G, nx, ny, rows, lanes), bf16),
            pltpu.VMEM((G, nx, ny, rows, lanes), bf16),
            pltpu.VMEM((G, nx, ny, rows, lanes), f32),
            pltpu.VMEM((G, nx, ny, rows, lanes), bf16),
            pltpu.VMEM((nx - 1, G, ny, rows, lanes), bf16),
            pltpu.VMEM((G, ny, rows, lanes), f32),
            pltpu.VMEM((G, ny, rows, lanes), bf16),
            pltpu.VMEM((ny - 1, G, rows, lanes), bf16),
            pltpu.VMEM((nz, SLOT, lanes), f32),
            pltpu.VMEM((nz - 1, SLOT, lanes), f32),
            pltpu.VMEM((SLOT, lanes), f32),
            pltpu.VMEM((2 * nx, SLOT, lanes), f32),
            dma((G,)), dma((G,)),
            dma((nx - 1, G)), dma((nx - 1, G)),
            dma((ny - 1, G)), dma((ny - 1, G)),
            dma((nz - 1,)), dma((nz - 1,)),
            dma((group,)), dma((group,)),
        ],
        compiler_params=pltpu.CompilerParams(
            collective_id=0, has_side_effects=True, vmem_limit_bytes=48 * 1024 * 1024
        ),
    )(parts)


def lay_out(grad_sub, grad_down, sizes):
    nx, ny, nz = sizes
    workers = 2 * nx
    lanes = grad_sub.shape[-1]
    sub = grad_sub.reshape(ny, nz, -1, lanes)
    sub = jnp.pad(sub, ((0, 0), (0, 0), (0, workers * SUB_W - sub.shape[2]), (0, 0)))
    sub = sub.reshape(ny, nz, workers, SUB_W, lanes)
    down = grad_down.reshape(ny, nz, workers, DOWN_W, lanes)
    both = jnp.concatenate([sub, down], axis=3)
    both = jnp.pad(both, ((0, 0), (0, 0), (0, 0), (0, ROW_W - SUB_W - DOWN_W), (0, 0)))
    both = both.reshape(ny, G, nz // G, 2, nx, ROW_W, lanes)
    both = jnp.transpose(both, (3, 1, 4, 0, 2, 5, 6))
    return both.reshape(2, G, nx, ny, nz // G * ROW_W, lanes)


def pick_share(whole, width_sub, width_down):
    core = lax.rem(lax.axis_index("tile"), 2)
    lanes = whole.shape[-1]
    rows_sub, rows_down = width_sub // lanes, width_down // lanes
    sub = whole[:, :SUB_W].reshape(-1, lanes)
    down = whole[:, SUB_W:SUB_W + DOWN_W].reshape(-1, lanes)
    sub = jnp.where(core == 0, sub[:rows_sub], sub[rows_sub:2 * rows_sub])
    down = jnp.where(core == 0, down[:rows_down], down[rows_down:2 * rows_down])
    return sub.reshape(-1), down.reshape(-1)


def with_halo(x, sides, width):
    for axis, dim in sides:
        size, length = (lax.axis_size(axis), x.shape[dim])
        up = [(i, (i + 1) % size) for i in range(size - 1)]
        down = [(j, i) for i, j in up]
        last = lax.slice_in_dim(x, length - width, length, axis=dim)
        first = lax.slice_in_dim(x, 0, width, axis=dim)
        before = lax.ppermute(last, axis, up)
        after = lax.ppermute(first, axis, down)
        x = jnp.concatenate([before, x, after], axis=dim)
    return x


def to_children(fine_blocks):
    count, voxels, channels = fine_blocks.shape
    half_depth = voxels // 32
    shaped = fine_blocks.reshape(count, half_depth, 2, 2, 2, 2, 2, channels)
    shaped = jnp.transpose(shaped, (0, 2, 4, 6, 1, 3, 5, 7))
    return shaped.reshape(count, 8, voxels // 8, channels)


def from_children(child_blocks):
    count, eight, places, channels = child_blocks.shape
    half_depth = places // 4
    shaped = child_blocks.reshape(count, 2, 2, 2, half_depth, 2, 2, channels)
    shaped = jnp.transpose(shaped, (0, 4, 1, 5, 2, 6, 3, 7))
    return shaped.reshape(count, places * 8, channels)


def octants_to_block(octant_blocks):
    count, eight, places, channels = octant_blocks.shape
    half_depth = places // 4
    shaped = octant_blocks.reshape(count, 2, 2, 2, half_depth, 2, 2, channels)
    shaped = jnp.transpose(shaped, (0, 1, 4, 2, 5, 3, 6, 7))
    return shaped.reshape(count, places * 8, channels)


def block_to_octants(coarse_blocks):
    count, voxels, channels = coarse_blocks.shape
    half_depth = voxels // 32
    shaped = coarse_blocks.reshape(count, 2, half_depth, 2, 2, 2, 2, channels)
    shaped = jnp.transpose(shaped, (0, 1, 3, 5, 2, 4, 6, 7))
    return shaped.reshape(count, 8, voxels // 8, channels)


def return_terms(voxel_pick, block_pick, grads_bf, weights_f):
    spread = jnp.einsum("bkvu,bvd->bkud", voxel_pick, grads_bf, preferred_element_type=jnp.float32)
    terms = jnp.einsum("bkud,kcd->bkuc", spread, weights_f, precision=lax.Precision.HIGHEST)
    return jnp.einsum(
        "bke,bkuc->euc", block_pick.astype(jnp.float32), terms, precision=lax.Precision.HIGHEST
    )


def on_device(
    features,
    w_sub,
    w_down,
    cotangent,
    vox_mask,
    nbr_owner,
    nbr_slot,
    voxel_map,
    parent_slot,
    parent_octant,
):
    blocks = features.shape[1]
    voxels = features.shape[2]
    channels = features.shape[3]
    coarse_count = cotangent.shape[1]
    tile_index = lax.axis_index("tile")
    active = vox_mask[0] > 0
    keep_f = active.reshape(-1, 1).astype(jnp.float32)
    masked = jnp.where(active[:, :, None], features[0], jnp.zeros((), jnp.bfloat16))
    halo_width = FACE
    extended = with_halo(masked, (("tile", 0),), halo_width)
    ext_count = extended.shape[0]
    owner_tile = nbr_owner[0]
    slot_index = nbr_slot[0]
    position = jnp.where(
        owner_tile == tile_index - 1,
        slot_index - (blocks - halo_width),
        jnp.where(
            owner_tile == tile_index, halo_width + slot_index, halo_width + blocks + slot_index
        ),
    )
    block_pick = (
        (position[:, :, None] == jnp.arange(ext_count, dtype=jnp.int32)[None, None, :])
        & (owner_tile >= 0)[:, :, None]
    ).astype(jnp.bfloat16)
    voxel_pick = (
        voxel_map[0][:, :, :, None] == jnp.arange(voxels, dtype=jnp.int32)[None, None, None, :]
    ).astype(jnp.bfloat16)
    source_blocks = jnp.einsum(
        "bke,euc->bkuc", block_pick, extended, preferred_element_type=jnp.float32
    ).astype(jnp.bfloat16)
    gathered = jnp.einsum(
        "bkvu,bkuc->bkvc", voxel_pick, source_blocks, preferred_element_type=jnp.float32
    ).astype(jnp.bfloat16)
    pre_act = jnp.einsum(
        "bkvc,kcd->bvd", gathered, w_sub, preferred_element_type=jnp.float32
    ).reshape(-1, channels)
    hidden = (keep_f * jax.nn.silu(pre_act)).astype(jnp.bfloat16)
    children = to_children(hidden.reshape(blocks, voxels, channels))
    parent_pick = (
        parent_slot[0][:, None, None] == jnp.arange(coarse_count, dtype=jnp.int32)[None, :, None]
    ) & (parent_octant[0][:, None, None] == jnp.arange(8, dtype=jnp.int32)[None, None, :])
    partial_value = jnp.einsum(
        "ncuk,ckj->nuj", children, w_down, preferred_element_type=jnp.float32
    )
    coarse_oct = jnp.einsum(
        "nqo,nuj->qouj",
        parent_pick.astype(jnp.float32),
        partial_value,
        precision=lax.Precision.HIGHEST,
    )
    coarse_out = octants_to_block(coarse_oct).astype(jnp.bfloat16)[None]
    cot_oct = block_to_octants(cotangent[0])
    picked = jnp.einsum(
        "nqo,qouj->nuj",
        parent_pick.astype(jnp.bfloat16),
        cot_oct,
        preferred_element_type=jnp.float32,
    ).astype(jnp.bfloat16)
    dchildren = jnp.einsum("nuj,ckj->ncuk", picked, w_down, preferred_element_type=jnp.float32)
    grad_down = jnp.einsum("ncuk,nuj->ckj", children, picked, preferred_element_type=jnp.float32)
    dhidden = from_children(dchildren).reshape(-1, channels)
    sigmoid_pre = jax.nn.sigmoid(pre_act)
    dpre = (keep_f * dhidden * sigmoid_pre * (1.0 + pre_act * (1.0 - sigmoid_pre))).astype(
        jnp.bfloat16
    )
    dpre_blocks = dpre.reshape(blocks, voxels, channels)
    grad_sub = jnp.einsum(
        "bkvc,bvd->kcd", gathered, dpre_blocks, preferred_element_type=jnp.float32
    )
    weights_f = w_sub.astype(jnp.float32)
    grad_rows = return_terms(voxel_pick, block_pick, dpre_blocks, weights_f)
    own_grad = grad_rows[halo_width : halo_width + blocks]
    outgoing = jnp.concatenate([grad_rows[:halo_width], grad_rows[halo_width + blocks :]], axis=0)
    returned = with_halo(outgoing.astype(jnp.bfloat16), (("tile", 0),), halo_width).astype(
        outgoing.dtype
    )
    own_grad = own_grad.at[:halo_width].add(returned[:halo_width])
    own_grad = own_grad.at[blocks - halo_width :].add(returned[3 * halo_width :])
    grad_input = (keep_f.reshape(blocks, voxels, 1) * own_grad).astype(jnp.bfloat16)[None]
    grad_scale = float(lax.axis_size("dp") * lax.axis_size("tile") * blocks * voxels) ** (-0.5)
    sizes = (lax.axis_size("dp"), 8, lax.axis_size("tile") // 16)
    width_sub = grad_sub.size // lax.axis_size("tile")
    width_down = grad_down.size // lax.axis_size("tile")
    whole = reduce_parts(lay_out(grad_sub, grad_down, sizes), sizes, grad_scale)
    share_sub, share_down = pick_share(whole, width_sub, width_down)
    return (coarse_out, grad_input, share_sub, share_down)


def solution(mesh):
    in_specs = (
        P("dp", "tile", None, None),
        P(),
        P(),
        P("dp", "tile", None, None),
        P("dp", "tile", None),
        P("dp", "tile", None),
        P("dp", "tile", None),
        P("dp", "tile", None, None),
        P("dp", "tile"),
        P("dp", "tile"),
    )
    out_specs = (P("dp", "tile", None, None), P("dp", "tile", None, None), P("tile"), P("tile"))
    return jax.shard_map(
        on_device, mesh=mesh, in_specs=in_specs, out_specs=out_specs, check_vma=False
    )
```

```python
import functools

import jax
import jax.numpy as jnp
from jax import lax
from jax.experimental import pallas as pl
from jax.experimental.pallas import tpu as pltpu
from jax.sharding import PartitionSpec as P

FACE = 2
MESH = pl.DeviceIdType.MESH


def with_halo(x, sides, width):
    for axis, dim in sides:
        size, length = (lax.axis_size(axis), x.shape[dim])
        up = [(i, (i + 1) % size) for i in range(size - 1)]
        down = [(j, i) for i, j in up]
        last = lax.slice_in_dim(x, length - width, length, axis=dim)
        first = lax.slice_in_dim(x, 0, width, axis=dim)
        before = lax.ppermute(last, axis, up)
        after = lax.ppermute(first, axis, down)
        x = jnp.concatenate([before, x, after], axis=dim)
    return x


TILE_ROWS = 8
SUB_T, DOWN_T = 7, 4
CHUNK_T = 6


def child_order(shape):
    new = lax.broadcasted_iota(jnp.int32, shape, 1)
    child, place = new // 16, new % 16
    z = 2 * (place // 4) + child // 4
    y = 2 * ((place // 2) % 2) + (child // 2) % 2
    x = 2 * (place % 2) + child % 2
    return 16 * z + 4 * y + x


def local_kernel(
    sizes, pos_ref, ext_ref, map_ref, ws_ref, wd_ref, cot_ref, mask_ref, tgt_ref,
    coarse_ref, acc_ref, parts_ref,
    picks, gathered, ext_t, ws_t, map_p, pre_t, hidden, factor, dpre, pairs, grad_sub, grad_down,
):
    f32, bf16 = jnp.float32, jnp.bfloat16
    offsets, voxels, wide = picks.shape
    blocks = wide // voxels
    channels = ws_ref.shape[1]

    def dot(a, b, dims=((1,), (0,))):
        return lax.dot_general(a, b, (dims, ((), ())), preferred_element_type=f32)

    lanes = lambda b: pl.ds(b * voxels, voxels)
    perm = (
        lax.broadcasted_iota(jnp.int32, (voxels, voxels), 0) == child_order((voxels, voxels))
    ).astype(bf16)
    for e in range(ext_ref.shape[0]):
        ext_t[e] = ext_ref[e].T
    map_p[...] = dot(map_ref[...].astype(bf16), perm)
    keep = dot(mask_ref[...].astype(bf16), perm)
    row_ids = lax.broadcasted_iota(jnp.int32, (voxels, voxels), 0).astype(f32)

    def forward(k, c):
        ws_t[:, pl.ds(pl.multiple_of(k * channels, channels), channels)] = ws_ref[k].T
        rows = map_p[pl.ds(pl.multiple_of(k * blocks, blocks), blocks), :]
        for b in range(blocks):
            e = pos_ref[b, k]
            row = rows[b:b + 1] - jnp.where(e < 0, 1000.0, 0.0)
            tile = (row_ids == row).astype(bf16)
            picks[k, :, lanes(b)] = tile
            gathered[k, :, lanes(b)] = dot(ext_t[jnp.maximum(e, 0)], tile).astype(bf16)
        return c

    lax.fori_loop(0, offsets, forward, 0)

    flat = gathered.reshape(offsets * voxels, wide)
    for p in range(blocks // 2):
        cols = pl.ds(p * 2 * voxels, 2 * voxels)
        pre_t[:, cols] = dot(ws_t[...], flat[:, cols])
    for b in range(blocks):
        pre = pre_t[:, lanes(b)]
        sig = jax.nn.sigmoid(pre)
        keep_b = keep[b:b + 1]
        hid = (keep_b * (pre * sig)).T.astype(bf16)
        for c in range(8):
            hidden[b * 16:(b + 1) * 16, c * channels:(c + 1) * channels] = hid[c * 16:(c + 1) * 16]
        factor[lanes(b), :] = (keep_b * sig * (1.0 + pre * (1.0 - sig))).T
    scatter = (
        lax.broadcasted_iota(jnp.int32, (cot_ref.shape[0], tgt_ref.shape[1]), 0) == tgt_ref[...]
    ).astype(bf16)
    partial_value = dot(hidden[...], wd_ref[...]).astype(bf16)
    coarse_ref[...] = dot(scatter, partial_value).astype(bf16)
    picked = dot(scatter, cot_ref[...], ((0,), (0,))).astype(bf16)
    dchildren = dot(picked, wd_ref[...], ((1,), (1,)))
    grad_down[...] = dot(hidden[...], picked, ((0,), (0,)))
    pairs[...] = jnp.zeros_like(pairs)
    for b in range(blocks):
        for c in range(8):
            rows = slice(b * voxels + c * 16, b * voxels + (c + 1) * 16)
            part = dchildren[b * 16:(b + 1) * 16, c * channels:(c + 1) * channels]
            dpre[rows, :] = (part * factor[rows, :]).astype(bf16)
        half = (b % 2) * voxels
        pairs[b // 2, half:half + voxels, half:half + voxels] = dpre[lanes(b), :]

    acc_ref[...] = jnp.zeros_like(acc_ref)

    def backward(k, c):
        at = pl.ds(pl.multiple_of(k * channels, channels), channels)
        grad_sub[at, :] = dot(gathered[k], dpre[...])
        weight = ws_ref[k]
        for p in range(blocks // 2):
            spread = dot(picks[k, :, pl.ds(p * 2 * voxels, 2 * voxels)], pairs[p]).astype(bf16)
            for i in range(2):
                e = jnp.maximum(pos_ref[2 * p + i, k], 0)
                term = dot(spread[:, i * channels:(i + 1) * channels], weight, ((1,), (1,)))
                acc_ref[e] += term
        return c

    lax.fori_loop(0, offsets, backward, 0)

    nx, ny, nz = sizes
    grad_sub[offsets * channels:, :] = jnp.zeros((TILE_ROWS, channels), f32)
    chip_rows = offsets * channels // (ny * nz)
    for y in range(ny):
        for z in range(nz):
            for i in range(SUB_T + DOWN_T):
                order = z * (SUB_T + DOWN_T) + i
                w, p = order % (2 * nx), order // (2 * nx)
                if i < SUB_T:
                    start = (y * nz + z) * chip_rows + i * TILE_ROWS
                    tile = grad_sub[start:start + TILE_ROWS, :]
                else:
                    m = i - SUB_T
                    start = y * 128 + z * 16 + (m % 2) * TILE_ROWS
                    tile = grad_down[start:start + TILE_ROWS, (m // 2) * 128:(m // 2 + 1) * 128]
                row = (p % CHUNK_T) * TILE_ROWS
                parts_ref[w // nx, p // CHUNK_T, w % nx, y, row:row + TILE_ROWS, :] = tile
    for w in range(2 * nx):
        row = (CHUNK_T - 1) * TILE_ROWS
        for y in range(ny):
            parts_ref[w // nx, G - 1, w % nx, y, row:row + TILE_ROWS, :] = jnp.zeros(
                (TILE_ROWS, 128), f32
            )


def local_pass(pos, ext, voxel_map, w_sub, w_down, cot, mask, tgt, sizes):
    nx, ny, nz = sizes
    offsets, channels, _ = w_sub.shape
    blocks, voxels = mask.shape
    f32, bf16 = jnp.float32, jnp.bfloat16
    wide = blocks * voxels
    vmem = pl.BlockSpec(memory_space=pltpu.VMEM)
    return pl.pallas_call(
        functools.partial(local_kernel, sizes),
        out_shape=(
            jax.ShapeDtypeStruct((cot.shape[0], cot.shape[1]), bf16),
            jax.ShapeDtypeStruct(ext.shape, f32),
            jax.ShapeDtypeStruct((2, G, nx, ny, CHUNK_T * TILE_ROWS, 128), f32),
        ),
        in_specs=[pl.BlockSpec(memory_space=pltpu.SMEM)] + [vmem] * 7,
        out_specs=(vmem,) * 3,
        scratch_shapes=[
            pltpu.VMEM((offsets, voxels, wide), bf16),
            pltpu.VMEM((offsets, channels, wide), bf16),
            pltpu.VMEM((ext.shape[0], channels, voxels), bf16),
            pltpu.VMEM((channels, offsets * channels), bf16),
            pltpu.VMEM((offsets * blocks, voxels), f32),
            pltpu.VMEM((channels, wide), f32),
            pltpu.VMEM((wide // 8, 8 * channels), bf16),
            pltpu.VMEM((wide, channels), f32),
            pltpu.VMEM((wide, channels), bf16),
            pltpu.VMEM((blocks // 2, 2 * voxels, 2 * channels), bf16),
            pltpu.VMEM((offsets * channels + TILE_ROWS, channels), f32),
            pltpu.VMEM((8 * channels, cot.shape[1]), f32),
        ],
        compiler_params=pltpu.CompilerParams(vmem_limit_bytes=56 * 1024 * 1024),
    )(pos, ext, voxel_map, w_sub, w_down, cot, mask, tgt)


G = 2
SLOT = 16


def reduce_kernel(
    sizes, scale, parts_ref, sub_ref, down_ref, send0, recv0, acc1, send1, recv1, acc2, send2, recv2,
    tiles, recv3, fin, gath, share, ss0, rs0, ss1, rs1, ss2, rs2, ss3, rs3, ss4, rs4,
):
    nx, ny, nz = sizes
    workers = 2 * nx
    per_chip = SUB_T + DOWN_T
    tile = lax.axis_index("tile")
    x = lax.axis_index("dp")
    core = lax.rem(tile, 2)
    z = lax.rem(tile // 2, nz)
    y = tile // (2 * nz)
    other = 1 - core
    f32, bf16 = jnp.float32, jnp.bfloat16

    def place(yy, zz, cc):
        return (yy * nz + zz) * 2 + cc

    x_peers = [lax.rem(x + d, nx) for d in range(1, nx)]
    y_peers = [lax.rem(y + d, ny) for d in range(1, ny)]
    z_peers = [lax.rem(z + d, nz) for d in range(1, nz)]
    group = [(f, d) for f in (0, 1) for d in range(nx) if (f, d) != (0, 0)]

    def worker(f, d):
        cc = core if f == 0 else other
        return cc, lax.rem(x + d, nx)

    barrier = pltpu.get_barrier_semaphore()
    for f, d in group:
        cc, xx = worker(f, d)
        pl.semaphore_signal(barrier, inc=1, device_id=(place(y, z, cc), xx), device_id_type=MESH)
    for yy in y_peers:
        pl.semaphore_signal(barrier, inc=1, device_id=(place(yy, z, core), x), device_id_type=MESH)
    for zz in z_peers:
        pl.semaphore_signal(barrier, inc=1, device_id=(place(y, zz, core), x), device_id_type=MESH)

    copies = []

    def send(src, dst, ss, rs, t, xx):
        copy = pltpu.make_async_remote_copy(
            src_ref=src, dst_ref=dst, send_sem=ss, recv_sem=rs,
            device_id=(t, xx), device_id_type=MESH,
        )
        copy.start()
        copies.append(copy)
        return copy

    def cast_half(g):
        def body(i, c):
            send0[g, i] = parts_ref[other, g, i].astype(bf16)
            return c
        lax.fori_loop(0, nx, body, 0)

    cast_half(0)
    pl.semaphore_wait(barrier, len(group) + ny - 1 + nz - 1)
    step0 = []
    for g in range(G):
        if g:
            cast_half(g)
        step0.append(send(send0.at[g], recv0.at[g], ss0.at[g], rs0.at[g], place(y, z, other), x))

    step1 = []
    for g in range(G):
        step0[g].wait_recv()

        def body(i, c):
            total = parts_ref[core, g, i] + recv0[g, i].astype(f32)
            acc1[g, i] = total
            send1[g, i] = total.astype(bf16)
            return c

        lax.fori_loop(0, nx, body, 0)
        step1.append([
            send(send1.at[g, xx], recv1.at[d, g], ss1.at[d, g], rs1.at[d, g], tile, xx)
            for d, xx in enumerate(x_peers)
        ])

    step2 = []
    for g in range(G):
        for copy in step1[g]:
            copy.wait_recv()

        def body(i, c):
            total = acc1[g, x, i]
            for d in range(nx - 1):
                total = total + recv1[d, g, i].astype(f32)
            acc2[g, i] = total
            send2[g, i] = total.astype(bf16)
            return c

        lax.fori_loop(0, ny, body, 0)
        step2.append([
            send(send2.at[g, yy], recv2.at[d, g], ss2.at[d, g], rs2.at[d, g], place(yy, z, core), x)
            for d, yy in enumerate(y_peers)
        ])

    for g in range(G):
        for copy in step2[g]:
            copy.wait_recv()
        total = acc2[g, y]
        for d in range(ny - 1):
            total = total + recv2[d, g].astype(f32)
        for j in range(CHUNK_T):
            tiles[g * CHUNK_T + j] = total[j * TILE_ROWS:(j + 1) * TILE_ROWS]
    tiles[G * CHUNK_T] = jnp.zeros((TILE_ROWS, 128), f32)

    mine = core * nx + x

    def first_tile(zz):
        begin = zz * per_chip
        return (begin + lax.rem(mine + per_chip * workers * nz - begin, workers)) // workers

    step3 = [
        send(
            tiles.at[pl.ds(first_tile(zz), 2)], recv3.at[d], ss3.at[d], rs3.at[d],
            place(y, zz, core), x,
        )
        for d, zz in enumerate(z_peers)
    ]
    own = first_tile(z)
    for copy in step3:
        copy.wait_recv()
    for j in range(2):
        total = tiles[own + j]
        for d in range(nz - 1):
            total = total + recv3[d, j]
        fin[j] = total * scale
    step4 = []
    for i, (f, d) in enumerate(group):
        cc, xx = worker(f, d)
        step4.append(send(fin, gath.at[mine], ss4.at[i], rs4.at[i], place(y, z, cc), xx))
    gath[mine] = fin[...]
    for copy in step4:
        copy.wait_recv()
    begin = z * per_chip
    for i in range(SUB_T):
        share[i * TILE_ROWS:(i + 1) * TILE_ROWS, :] = gath[lax.rem(begin + i, workers), i // workers]
    rows = sub_ref.shape[0]
    low, high = share[0:rows, :], share[rows:2 * rows, :]
    pick = (core == 0).astype(f32)
    sub_ref[...] = low * pick + high * (1.0 - pick)
    for h in range(2):
        both = [
            gath[lax.rem(begin + SUB_T + 2 * h + j, workers), (SUB_T + 2 * h + j) // workers]
            for j in range(2)
        ]
        down_ref[:, h * 128:(h + 1) * 128] = both[0] * pick + both[1] * (1.0 - pick)
    for copy in copies:
        copy.wait_send()


def reduce_parts(parts, sizes, scale, sub_rows):
    nx, ny, nz = sizes
    rows = parts.shape[4]
    f32, bf16 = jnp.float32, jnp.bfloat16
    dma = pltpu.SemaphoreType.DMA
    lanes = parts.shape[5]
    group = 2 * nx - 1
    vmem = pl.BlockSpec(memory_space=pltpu.VMEM)
    return pl.pallas_call(
        functools.partial(reduce_kernel, sizes, scale),
        out_shape=(
            jax.ShapeDtypeStruct((sub_rows, lanes), f32),
            jax.ShapeDtypeStruct((TILE_ROWS, 2 * lanes), f32),
        ),
        in_specs=[vmem],
        out_specs=(vmem, vmem),
        scratch_shapes=[
            pltpu.VMEM((G, nx, ny, rows, lanes), bf16),
            pltpu.VMEM((G, nx, ny, rows, lanes), bf16),
            pltpu.VMEM((G, nx, ny, rows, lanes), f32),
            pltpu.VMEM((G, nx, ny, rows, lanes), bf16),
            pltpu.VMEM((nx - 1, G, ny, rows, lanes), bf16),
            pltpu.VMEM((G, ny, rows, lanes), f32),
            pltpu.VMEM((G, ny, rows, lanes), bf16),
            pltpu.VMEM((ny - 1, G, rows, lanes), bf16),
            pltpu.VMEM((G * CHUNK_T + 1, TILE_ROWS, lanes), f32),
            pltpu.VMEM((nz - 1, 2, TILE_ROWS, lanes), f32),
            pltpu.VMEM((2, TILE_ROWS, lanes), f32),
            pltpu.VMEM((2 * nx, 2, TILE_ROWS, lanes), f32),
            pltpu.VMEM((SUB_T * TILE_ROWS, lanes), f32),
            dma((G,)), dma((G,)),
            dma((nx - 1, G)), dma((nx - 1, G)),
            dma((ny - 1, G)), dma((ny - 1, G)),
            dma((nz - 1,)), dma((nz - 1,)),
            dma((group,)), dma((group,)),
        ],
        compiler_params=pltpu.CompilerParams(
            collective_id=0, has_side_effects=True, vmem_limit_bytes=48 * 1024 * 1024
        ),
    )(parts)


def on_device(
    features,
    w_sub,
    w_down,
    cotangent,
    vox_mask,
    nbr_owner,
    nbr_slot,
    voxel_map,
    parent_slot,
    parent_octant,
):
    blocks = features.shape[1]
    voxels = features.shape[2]
    channels = features.shape[3]
    coarse_count = cotangent.shape[1]
    tile_index = lax.axis_index("tile")
    active = vox_mask[0] > 0
    keep_f = active.reshape(-1, 1).astype(jnp.float32)
    masked = jnp.where(active[:, :, None], features[0], jnp.zeros((), jnp.bfloat16))
    halo_width = FACE
    extended = with_halo(masked, (("tile", 0),), halo_width)
    ext_count = extended.shape[0]
    owner_tile = nbr_owner[0]
    slot_index = nbr_slot[0]
    position = jnp.where(
        owner_tile == tile_index - 1,
        slot_index - (blocks - halo_width),
        jnp.where(
            owner_tile == tile_index, halo_width + slot_index, halo_width + blocks + slot_index
        ),
    )
    position = jnp.where(owner_tile >= 0, position, -1)
    sizes = (lax.axis_size("dp"), 8, lax.axis_size("tile") // 16)
    maps = jnp.transpose(voxel_map[0], (1, 0, 2)).reshape(-1, voxels)
    place = jnp.arange(16, dtype=jnp.int32)[None, :]
    octant = parent_octant[0][:, None]
    within = (
        16 * (4 * (octant // 4) + place // 4)
        + 4 * (2 * ((octant // 2) % 2) + (place // 2) % 2)
        + 2 * (octant % 2) + place % 2
    )
    target = (parent_slot[0][:, None] * cotangent.shape[2] + within).reshape(1, -1)
    coarse, grad_rows, parts = local_pass(
        position, extended, maps, w_sub, w_down.reshape(-1, w_down.shape[2]),
        cotangent[0].reshape(-1, cotangent.shape[3]), vox_mask[0], target, sizes,
    )
    coarse_out = coarse.reshape(cotangent.shape)
    own_grad = grad_rows[halo_width : halo_width + blocks]
    outgoing = jnp.concatenate([grad_rows[:halo_width], grad_rows[halo_width + blocks :]], axis=0)
    returned = with_halo(outgoing.astype(jnp.bfloat16), (("tile", 0),), halo_width).astype(
        outgoing.dtype
    )
    own_grad = own_grad.at[:halo_width].add(returned[:halo_width])
    own_grad = own_grad.at[blocks - halo_width :].add(returned[3 * halo_width :])
    grad_input = (keep_f.reshape(blocks, voxels, 1) * own_grad).astype(jnp.bfloat16)[None]
    grad_scale = float(lax.axis_size("dp") * lax.axis_size("tile") * blocks * voxels) ** (-0.5)
    sub_rows = w_sub.size // channels // lax.axis_size("tile")
    share_sub, share_down = reduce_parts(parts, sizes, grad_scale, sub_rows)
    return (coarse_out, grad_input, share_sub.reshape(-1), share_down.reshape(-1))


def solution(mesh):
    in_specs = (
        P("dp", "tile", None, None),
        P(),
        P(),
        P("dp", "tile", None, None),
        P("dp", "tile", None),
        P("dp", "tile", None),
        P("dp", "tile", None),
        P("dp", "tile", None, None),
        P("dp", "tile"),
        P("dp", "tile"),
    )
    out_specs = (P("dp", "tile", None, None), P("dp", "tile", None, None), P("tile"), P("tile"))
    return jax.shard_map(
        on_device, mesh=mesh, in_specs=in_specs, out_specs=out_specs, check_vma=False
    )
```

```python
import functools

import jax
import jax.numpy as jnp
from jax import lax
from jax.experimental import pallas as pl
from jax.experimental.pallas import tpu as pltpu
from jax.sharding import PartitionSpec as P

FACE = 2
MESH = pl.DeviceIdType.MESH


def with_halo(x, sides, width):
    for axis, dim in sides:
        size, length = (lax.axis_size(axis), x.shape[dim])
        up = [(i, (i + 1) % size) for i in range(size - 1)]
        down = [(j, i) for i, j in up]
        last = lax.slice_in_dim(x, length - width, length, axis=dim)
        first = lax.slice_in_dim(x, 0, width, axis=dim)
        before = lax.ppermute(last, axis, up)
        after = lax.ppermute(first, axis, down)
        x = jnp.concatenate([before, x, after], axis=dim)
    return x


TILE_ROWS = 8
HALF_T = 3


def child_order(shape):
    new = lax.broadcasted_iota(jnp.int32, shape, 1)
    child, place = new // 16, new % 16
    z = 2 * (place // 4) + child // 4
    y = 2 * ((place // 2) % 2) + (child // 2) % 2
    x = 2 * (place % 2) + child % 2
    return 16 * z + 4 * y + x


def local_kernel(
    sizes, pos_ref, ext_ref, map_ref, ws_ref, wd_ref, cot_ref, mask_ref, tgt_ref,
    coarse_ref, acc_ref, parts_ref,
    picks, gathered, ext_t, ws_t, map_p, pre_t, hidden, factor, dpre, pairs, grad_sub, grad_down,
):
    f32, bf16 = jnp.float32, jnp.bfloat16
    offsets, voxels, wide = picks.shape
    blocks = wide // voxels
    channels = ws_ref.shape[1]

    def dot(a, b, dims=((1,), (0,))):
        return lax.dot_general(a, b, (dims, ((), ())), preferred_element_type=f32)

    lanes = lambda b: pl.ds(b * voxels, voxels)
    perm = (
        lax.broadcasted_iota(jnp.int32, (voxels, voxels), 0) == child_order((voxels, voxels))
    ).astype(bf16)
    for e in range(ext_ref.shape[0]):
        ext_t[e] = ext_ref[e].T
    map_p[...] = dot(map_ref[...].astype(bf16), perm)
    keep = dot(mask_ref[...].astype(bf16), perm)
    row_ids = lax.broadcasted_iota(jnp.int32, (voxels, voxels), 0).astype(f32)

    def forward(k, c):
        ws_t[:, pl.ds(pl.multiple_of(k * channels, channels), channels)] = ws_ref[k].T
        rows = map_p[pl.ds(pl.multiple_of(k * blocks, blocks), blocks), :]
        for b in range(blocks):
            e = pos_ref[b, k]
            row = rows[b:b + 1] - jnp.where(e < 0, 1000.0, 0.0)
            tile = (row_ids == row).astype(bf16)
            picks[k, :, lanes(b)] = tile
            gathered[k, :, lanes(b)] = dot(ext_t[jnp.maximum(e, 0)], tile).astype(bf16)
        return c

    lax.fori_loop(0, offsets, forward, 0, unroll=3)

    flat = gathered.reshape(offsets * voxels, wide)
    for p in range(blocks // 2):
        cols = pl.ds(p * 2 * voxels, 2 * voxels)
        pre_t[:, cols] = dot(ws_t[...], flat[:, cols])
    for b in range(blocks):
        pre = pre_t[:, lanes(b)]
        sig = jax.nn.sigmoid(pre)
        keep_b = keep[b:b + 1]
        hid = (keep_b * (pre * sig)).T.astype(bf16)
        for c in range(8):
            hidden[b * 16:(b + 1) * 16, c * channels:(c + 1) * channels] = hid[c * 16:(c + 1) * 16]
        factor[lanes(b), :] = (keep_b * sig * (1.0 + pre * (1.0 - sig))).T
    scatter = (
        lax.broadcasted_iota(jnp.int32, (cot_ref.shape[0], tgt_ref.shape[1]), 0) == tgt_ref[...]
    ).astype(bf16)
    partial_value = dot(hidden[...], wd_ref[...]).astype(bf16)
    coarse_ref[...] = dot(scatter, partial_value).astype(bf16)
    picked = dot(scatter, cot_ref[...], ((0,), (0,))).astype(bf16)
    dchildren = dot(picked, wd_ref[...], ((1,), (1,)))
    grad_down[...] = dot(hidden[...], picked, ((0,), (0,)))
    pairs[...] = jnp.zeros_like(pairs)
    for b in range(blocks):
        for c in range(8):
            rows = slice(b * voxels + c * 16, b * voxels + (c + 1) * 16)
            part = dchildren[b * 16:(b + 1) * 16, c * channels:(c + 1) * channels]
            dpre[rows, :] = (part * factor[rows, :]).astype(bf16)
        half = (b % 2) * voxels
        pairs[b // 2, half:half + voxels, half:half + voxels] = dpre[lanes(b), :]

    acc_ref[...] = jnp.zeros_like(acc_ref)

    flat_picks = picks.reshape(offsets * voxels, wide)

    def backward(j, c):
        for q in range(3):
            k = j * 3 + q
            at = pl.ds(pl.multiple_of(k * channels, channels), channels)
            grad_sub[at, :] = dot(gathered[k], dpre[...])
        rows = pl.ds(pl.multiple_of(j * 3 * voxels, 128), 3 * voxels)
        for p in range(blocks // 2):
            spread = dot(flat_picks[rows, pl.ds(p * 2 * voxels, 2 * voxels)], pairs[p]).astype(bf16)
            for q in range(3):
                k = j * 3 + q
                weight = ws_t[:, pl.ds(pl.multiple_of(k * channels, channels), channels)]
                for i in range(2):
                    e = jnp.maximum(pos_ref[2 * p + i, k], 0)
                    acc_ref[e] += dot(spread[q*voxels:(q+1)*voxels, i * channels:(i + 1) * channels], weight)
        return c

    lax.fori_loop(0, offsets // 3, backward, 0)

    nx, ny, nz = sizes
    grad_sub[offsets * channels:, :] = jnp.zeros((TILE_ROWS, channels), f32)
    share = offsets * channels // (2 * ny * nz)
    for y in range(ny):
        for z in range(nz):
            for core in range(2):
                start = ((y * nz + z) * 2 + core) * share
                for i in range(HALF_T):
                    rows = slice(i * TILE_ROWS, (i + 1) * TILE_ROWS)
                    tile = grad_sub[start + i * TILE_ROWS:start + (i + 1) * TILE_ROWS, :]
                    parts_ref[core, 0, y, z, rows, :] = tile
                tile = grad_sub[start + HALF_T * TILE_ROWS:start + (HALF_T + 1) * TILE_ROWS, :]
                parts_ref[core, 1, z, y, 0:TILE_ROWS, :] = tile
                start = y * channels + (z * 2 + core) * TILE_ROWS
                for i in range(2):
                    rows = slice((i + 1) * TILE_ROWS, (i + 2) * TILE_ROWS)
                    tile = grad_down[start:start + TILE_ROWS, i * 128:(i + 1) * 128]
                    parts_ref[core, 1, z, y, rows, :] = tile


def local_pass(pos, ext, voxel_map, w_sub, w_down, cot, mask, tgt, sizes):
    nx, ny, nz = sizes
    offsets, channels, _ = w_sub.shape
    blocks, voxels = mask.shape
    f32, bf16 = jnp.float32, jnp.bfloat16
    wide = blocks * voxels
    vmem = pl.BlockSpec(memory_space=pltpu.VMEM)
    return pl.pallas_call(
        functools.partial(local_kernel, sizes),
        out_shape=(
            jax.ShapeDtypeStruct((cot.shape[0], cot.shape[1]), bf16),
            jax.ShapeDtypeStruct(ext.shape, f32),
            jax.ShapeDtypeStruct((2, 2, ny, nz, HALF_T * TILE_ROWS, 128), f32),
        ),
        in_specs=[pl.BlockSpec(memory_space=pltpu.SMEM)] + [vmem] * 7,
        out_specs=(vmem,) * 3,
        scratch_shapes=[
            pltpu.VMEM((offsets, voxels, wide), bf16),
            pltpu.VMEM((offsets, channels, wide), bf16),
            pltpu.VMEM((ext.shape[0], channels, voxels), bf16),
            pltpu.VMEM((channels, offsets * channels), bf16),
            pltpu.VMEM((offsets * blocks, voxels), f32),
            pltpu.VMEM((channels, wide), f32),
            pltpu.VMEM((wide // 8, 8 * channels), bf16),
            pltpu.VMEM((wide, channels), f32),
            pltpu.VMEM((wide, channels), bf16),
            pltpu.VMEM((blocks // 2, 2 * voxels, 2 * channels), bf16),
            pltpu.VMEM((offsets * channels + TILE_ROWS, channels), f32),
            pltpu.VMEM((8 * channels, cot.shape[1]), f32),
        ],
        compiler_params=pltpu.CompilerParams(vmem_limit_bytes=56 * 1024 * 1024),
    )(pos, ext, voxel_map, w_sub, w_down, cot, mask, tgt)


def reduce_kernel(
    sizes, scale, parts_ref, terms_ref, mask_ref, sub_ref, down_ref, grad_ref,
    send0, recv0, acc1, send1, recv1, acc2, recv2, recv3, share, out_b, out_a, in_b, in_a,
    ss0, rs0, ss1, rs1, ss2, rs2, ss3, rs3, ssh, rsh,
):
    nx, ny, nz = sizes
    tile = lax.axis_index("tile")
    x = lax.axis_index("dp")
    core = lax.rem(tile, 2)
    z = lax.rem(tile // 2, nz)
    y = tile // (2 * nz)
    other = 1 - core
    count = 2 * ny * nz
    f32, bf16 = jnp.float32, jnp.bfloat16

    def place(yy, zz, cc):
        return (yy * nz + zz) * 2 + cc

    x_peers = [lax.rem(x + d, nx) for d in range(1, nx)]
    y_peers = [lax.rem(y + d, ny) for d in range(1, ny)]
    z_peers = [lax.rem(z + d, nz) for d in range(1, nz)]
    after, before = lax.rem(tile + 1, count), lax.rem(tile + count - 1, count)

    barrier = pltpu.get_barrier_semaphore()
    peers = [(place(y, z, other), x), (after, x), (before, x)]
    peers += [(tile, xx) for xx in x_peers]
    peers += [(place(yy, z, core), x) for yy in y_peers]
    peers += [(place(y, zz, core), x) for zz in z_peers]
    for peer in peers:
        pl.semaphore_signal(barrier, inc=1, device_id=peer, device_id_type=MESH)

    copies = []

    def send(src, dst, ss, rs, t, xx):
        copy = pltpu.make_async_remote_copy(
            src_ref=src, dst_ref=dst, send_sem=ss, recv_sem=rs,
            device_id=(t, xx), device_id_type=MESH,
        )
        copy.start()
        copies.append(copy)
        return copy

    def cast_half(h):
        def body(i, c):
            send0[h, i] = parts_ref[other, h, i].astype(bf16)
            return c
        lax.fori_loop(0, ny, body, 0)

    blocks = grad_ref.shape[0]
    cast_half(0)
    pl.semaphore_wait(barrier, len(peers))
    step0 = [send(send0.at[0], recv0.at[0], ss0.at[0], rs0.at[0], place(y, z, other), x)]
    cast_half(1)
    step0.append(send(send0.at[1], recv0.at[1], ss0.at[1], rs0.at[1], place(y, z, other), x))
    out_b[...] = terms_ref[0:FACE].astype(bf16)
    out_a[...] = terms_ref[FACE + blocks:].astype(bf16)

    step1 = []
    for h in range(2):
        step0[h].wait_recv()

        def body(i, c):
            total = parts_ref[core, h, i] + recv0[h, i].astype(f32)
            acc1[h, i] = total
            send1[h, i] = total.astype(bf16)
            return c

        lax.fori_loop(0, ny, body, 0)
        for d in range(ny - 1):
            to = y_peers[d] if h == 0 else z_peers[d]
            t = place(to, z, core) if h == 0 else place(y, to, core)
            step1.append(send(send1.at[h, to], recv1.at[h, d], ss1.at[h, d], rs1.at[h, d], t, x))
    halo = [
        send(out_b, in_a, ssh.at[0], rsh.at[0], before, x),
        send(out_a, in_b, ssh.at[1], rsh.at[1], after, x),
    ]

    step2 = []
    for h in range(2):
        for copy in step1[h * (ny - 1):(h + 1) * (ny - 1)]:
            copy.wait_recv()
        mine = y if h == 0 else z

        def body(i, c):
            total = acc1[h, mine, i]
            for d in range(ny - 1):
                total = total + recv1[h, d, i].astype(f32)
            acc2[h, i] = total
            return c

        lax.fori_loop(0, nz, body, 0)
        for d in range(nz - 1):
            to = z_peers[d] if h == 0 else y_peers[d]
            t = place(y, to, core) if h == 0 else place(to, z, core)
            step2.append(send(acc2.at[h, to], recv2.at[h, d], ss2.at[h, d], rs2.at[h, d], t, x))

    for copy in halo:
        copy.wait_recv()
    keep = mask_ref[...].astype(f32)
    for b in range(blocks):
        total = terms_ref[FACE + b]
        if b < FACE:
            total = total + in_b[b].astype(f32)
        if b >= blocks - FACE:
            total = total + in_a[b - (blocks - FACE)].astype(f32)
        column = jnp.broadcast_to(keep[b:b + 1], total.shape).T
        grad_ref[b] = (column * total).astype(bf16)

    for h in range(2):
        for copy in step2[h * (nz - 1):(h + 1) * (nz - 1)]:
            copy.wait_recv()
        total = acc2[h, z if h == 0 else y]
        for d in range(nz - 1):
            total = total + recv2[h, d]
        share[h] = total
    recv3[x] = share[...]
    step3 = [
        send(share, recv3.at[x], ss3.at[d], rs3.at[d], tile, xx) for d, xx in enumerate(x_peers)
    ]
    for copy in step3:
        copy.wait_recv()
    total = recv3[0]
    for i in range(1, nx):
        total = total + recv3[i]
    total = total * scale
    rows = sub_ref.shape[0]
    half = total.shape[1]
    sub_ref[0:half, :] = total[0]
    sub_ref[half:rows, :] = total[1, 0:rows - half]
    down_ref[:, 0:128] = total[1, TILE_ROWS:2 * TILE_ROWS]
    down_ref[:, 128:256] = total[1, 2 * TILE_ROWS:3 * TILE_ROWS]
    for copy in copies:
        copy.wait_send()


def reduce_parts(parts, terms, mask, sizes, scale, sub_rows):
    nx, ny, nz = sizes
    rows, lanes = parts.shape[4:]
    voxels, channels = terms.shape[1:]
    f32, bf16 = jnp.float32, jnp.bfloat16
    dma = pltpu.SemaphoreType.DMA
    vmem = pl.BlockSpec(memory_space=pltpu.VMEM)
    face = (FACE, voxels, channels)
    return pl.pallas_call(
        functools.partial(reduce_kernel, sizes, scale),
        out_shape=(
            jax.ShapeDtypeStruct((sub_rows, lanes), f32),
            jax.ShapeDtypeStruct((TILE_ROWS, 2 * lanes), f32),
            jax.ShapeDtypeStruct((mask.shape[0], voxels, channels), bf16),
        ),
        in_specs=[vmem] * 3,
        out_specs=(vmem,) * 3,
        scratch_shapes=[
            pltpu.VMEM((2, ny, nz, rows, lanes), bf16),
            pltpu.VMEM((2, ny, nz, rows, lanes), bf16),
            pltpu.VMEM((2, ny, nz, rows, lanes), f32),
            pltpu.VMEM((2, ny, nz, rows, lanes), bf16),
            pltpu.VMEM((2, ny - 1, nz, rows, lanes), bf16),
            pltpu.VMEM((2, nz, rows, lanes), f32),
            pltpu.VMEM((2, nz - 1, rows, lanes), f32),
            pltpu.VMEM((nx, 2, rows, lanes), f32),
            pltpu.VMEM((2, rows, lanes), f32),
            pltpu.VMEM(face, bf16), pltpu.VMEM(face, bf16),
            pltpu.VMEM(face, bf16), pltpu.VMEM(face, bf16),
            dma((2,)), dma((2,)),
            dma((2, ny - 1)), dma((2, ny - 1)),
            dma((2, nz - 1)), dma((2, nz - 1)),
            dma((nx - 1,)), dma((nx - 1,)),
            dma((2,)), dma((2,)),
        ],
        compiler_params=pltpu.CompilerParams(
            collective_id=0, has_side_effects=True, vmem_limit_bytes=48 * 1024 * 1024
        ),
    )(parts, terms, mask)


def on_device(
    features,
    w_sub,
    w_down,
    cotangent,
    vox_mask,
    nbr_owner,
    nbr_slot,
    voxel_map,
    parent_slot,
    parent_octant,
):
    blocks = features.shape[1]
    voxels = features.shape[2]
    channels = features.shape[3]
    coarse_count = cotangent.shape[1]
    tile_index = lax.axis_index("tile")
    active = vox_mask[0] > 0
    masked = jnp.where(active[:, :, None], features[0], jnp.zeros((), jnp.bfloat16))
    halo_width = FACE
    extended = with_halo(masked, (("tile", 0),), halo_width)
    ext_count = extended.shape[0]
    owner_tile = nbr_owner[0]
    slot_index = nbr_slot[0]
    position = jnp.where(
        owner_tile == tile_index - 1,
        slot_index - (blocks - halo_width),
        jnp.where(
            owner_tile == tile_index, halo_width + slot_index, halo_width + blocks + slot_index
        ),
    )
    position = jnp.where(owner_tile >= 0, position, -1)
    sizes = (lax.axis_size("dp"), 8, lax.axis_size("tile") // 16)
    maps = jnp.transpose(voxel_map[0], (1, 0, 2)).reshape(-1, voxels)
    place = jnp.arange(16, dtype=jnp.int32)[None, :]
    octant = parent_octant[0][:, None]
    within = (
        16 * (4 * (octant // 4) + place // 4)
        + 4 * (2 * ((octant // 2) % 2) + (place // 2) % 2)
        + 2 * (octant % 2) + place % 2
    )
    target = (parent_slot[0][:, None] * cotangent.shape[2] + within).reshape(1, -1)
    coarse, grad_rows, parts = local_pass(
        position, extended, maps, w_sub, w_down.reshape(-1, w_down.shape[2]),
        cotangent[0].reshape(-1, cotangent.shape[3]), vox_mask[0], target, sizes,
    )
    coarse_out = coarse.reshape(cotangent.shape)
    grad_scale = float(lax.axis_size("dp") * lax.axis_size("tile") * blocks * voxels) ** (-0.5)
    sub_rows = w_sub.size // channels // lax.axis_size("tile")
    share_sub, share_down, grad_input = reduce_parts(
        parts, grad_rows, vox_mask[0], sizes, grad_scale, sub_rows
    )
    return (coarse_out, grad_input[None], share_sub.reshape(-1), share_down.reshape(-1))


def solution(mesh):
    in_specs = (
        P("dp", "tile", None, None),
        P(),
        P(),
        P("dp", "tile", None, None),
        P("dp", "tile", None),
        P("dp", "tile", None),
        P("dp", "tile", None),
        P("dp", "tile", None, None),
        P("dp", "tile"),
        P("dp", "tile"),
    )
    out_specs = (P("dp", "tile", None, None), P("dp", "tile", None, None), P("tile"), P("tile"))
    return jax.shard_map(
        on_device, mesh=mesh, in_specs=in_specs, out_specs=out_specs, check_vma=False
    )
```

```python
import functools

import jax
import jax.numpy as jnp
from jax import lax
from jax.experimental import pallas as pl
from jax.experimental.pallas import tpu as pltpu
from jax.sharding import PartitionSpec as P

FACE = 2
MESH = pl.DeviceIdType.MESH
TILE_ROWS = 8
HALF_T = 3
PITCH = 32
NO_BLOCK = 99
NO_VOXEL = 1000


def child_order(shape):
    new = lax.broadcasted_iota(jnp.int32, shape, 1)
    child, place = new // 16, new % 16
    z = 2 * (place // 4) + child // 4
    y = 2 * ((place // 2) % 2) + (child // 2) % 2
    x = 2 * (place % 2) + child % 2
    return 16 * z + 4 * y + x


def dot(a, b, dims=((1,), (0,))):
    return lax.dot_general(a, b, (dims, ((), ())), preferred_element_type=jnp.float32)


def sort_rows(e_row, count):
    wide = e_row.shape[1]
    square = (wide, wide)
    down = lax.broadcasted_iota(jnp.int32, square, 0)
    along = lax.broadcasted_iota(jnp.int32, square, 1)
    theirs = jnp.broadcast_to(e_row, square)
    mine = theirs.T

    def total(where, value=1):
        return jnp.sum(jnp.where(where, value, 0), axis=0, keepdims=True)

    rank = total((mine < theirs) | ((mine == theirs) & (down < along)))
    rank_down = jnp.broadcast_to(rank, square).T
    order = jnp.minimum(total(rank_down == along, down), count - 1)
    same = jnp.where(
        total(rank_down == along, mine) == total(rank_down == along - 1, mine), 1, 0
    )
    last = jnp.clip(total(mine <= along) - 1, 0, count - 1)
    some = jnp.minimum(total(mine == along), 1)
    return order, order // TILE_ROWS, same, last, some


def kernel(
    sizes, scale, table_ref, erow_ref, feat_ref, map_ref, ws_ref, wd_ref, cot_ref,
    mask_ref, coarse_ref, grad_ref, sub_ref, down_ref,
    picks, gathered, ext_t, halo_in, ws_t, ws_k, spread_v, map_p, pre_t, hidden, factor, dpre, pairs,
    grad_sub, grad_down, sort_v, sort_s, seg, parts,
    send0, recv0, acc1, send1, recv1, acc2, recv2, recv3, share, out_h, in_h,
    sort_sem, ss0, rs0, ss1, rs1, ss2, rs2, ss3, rs3, ssh, rsh, ssg, rsg,
):
    f32, bf16 = jnp.float32, jnp.bfloat16
    nx, ny, nz = sizes
    tile = lax.axis_index("tile")
    x = lax.axis_index("dp")
    core = lax.rem(tile, 2)
    z = lax.rem(tile // 2, nz)
    y = tile // (2 * nz)
    other = 1 - core
    count = 2 * ny * nz

    def place(yy, zz, cc):
        return (yy * nz + zz) * 2 + cc

    x_peers = [lax.rem(x + d, nx) for d in range(1, nx)]
    y_peers = [lax.rem(y + d, ny) for d in range(1, ny)]
    z_peers = [lax.rem(z + d, nz) for d in range(1, nz)]
    after, before = lax.rem(tile + 1, count), lax.rem(tile + count - 1, count)

    barrier = pltpu.get_barrier_semaphore()
    peers = [(place(y, z, other), x), (after, x), (before, x)]
    peers += [(tile, xx) for xx in x_peers]
    peers += [(place(yy, z, core), x) for yy in y_peers]
    peers += [(place(y, zz, core), x) for zz in z_peers]
    for peer in peers:
        pl.semaphore_signal(barrier, inc=1, device_id=peer, device_id_type=MESH)

    copies = []

    def send(src, dst, ss, rs, t, xx):
        copy = pltpu.make_async_remote_copy(
            src_ref=src, dst_ref=dst, send_sem=ss, recv_sem=rs,
            device_id=(t, xx), device_id_type=MESH,
        )
        copy.start()
        copies.append(copy)
        return copy

    offsets, voxels, wide = picks.shape
    blocks = wide // voxels
    channels = ws_ref.shape[1]
    lanes = lambda b: pl.ds(b * voxels, voxels)

    masks = mask_ref[...].astype(bf16)
    for b in range(blocks):
        ext_t[FACE + b] = feat_ref[b].T * masks[b:b + 1]
    pl.semaphore_wait(barrier, len(peers))
    halo = [
        send(ext_t.at[pl.ds(FACE, FACE)], halo_in.at[1], ssh.at[0], rsh.at[0], before, x),
        send(ext_t.at[pl.ds(blocks, FACE)], halo_in.at[0], ssh.at[1], rsh.at[1], after, x),
    ]
    sort_v[...] = jnp.zeros_like(sort_v)
    for i, row in enumerate(sort_rows(erow_ref[...], offsets * blocks)):
        sort_v[i:i + 1, :] = row
    sort_copy = pltpu.make_async_copy(sort_v, sort_s, sort_sem)
    sort_copy.start()

    perm = (
        lax.broadcasted_iota(jnp.int32, (voxels, voxels), 0) == child_order((voxels, voxels))
    ).astype(bf16)
    for b in range(blocks):
        map_p[b, 0:offsets, :] = dot(map_ref[b].astype(bf16), perm)
    keep = dot(masks, perm)
    row_ids = lax.broadcasted_iota(jnp.int32, (voxels, voxels), 0).astype(f32)

    def transpose_weight(k, c):
        weight = ws_ref[k].T
        ws_k[k] = weight
        ws_t[:, pl.ds(pl.multiple_of(k * channels, channels), channels)] = weight
        return c

    def gather(some, weights):
        def body(k, c):
            if weights:
                transpose_weight(k, c)
            for b in some:
                row = map_p[b, pl.ds(k, 1), :] - table_ref[blocks + b, k].astype(f32)
                tile_bk = (row_ids == row).astype(bf16)
                picks[k, :, lanes(b)] = tile_bk
                gathered[k, :, lanes(b)] = dot(ext_t[table_ref[b, k]], tile_bk).astype(bf16)
            return c
        lax.fori_loop(0, offsets, body, 0, unroll=3)

    gather(range(FACE, blocks - FACE), True)
    for copy in halo:
        copy.wait_recv()
    for i in range(FACE):
        ext_t[i] = halo_in[0, i]
        ext_t[FACE + blocks + i] = halo_in[1, i]
    gather(list(range(FACE)) + list(range(blocks - FACE, blocks)), False)

    flat_g = gathered.reshape(offsets * channels, wide)
    flat_p = picks.reshape(offsets * voxels, wide)
    for p in range(blocks // 2):
        cols = pl.ds(p * 2 * voxels, 2 * voxels)
        pre_t[:, cols] = dot(ws_t[...], flat_g[:, cols])
    for b in range(blocks):
        pre = pre_t[:, lanes(b)]
        sig = jax.nn.sigmoid(pre)
        keep_b = keep[b:b + 1]
        hid = (keep_b * (pre * sig)).T.astype(bf16)
        for c in range(8):
            hidden[b * 16:(b + 1) * 16, c * channels:(c + 1) * channels] = hid[c * 16:(c + 1) * 16]
        factor[lanes(b), :] = (keep_b * sig * (1.0 + pre * (1.0 - sig))).T

    lane = lax.broadcasted_iota(jnp.int32, (1, voxels), 1)
    spot = lane % 16
    target = 16 * (spot // 4) + 4 * ((spot // 2) % 2) + spot % 2
    for b in range(blocks):
        target = target + jnp.where(lane // 16 == b, table_ref[2 * blocks, b], 0)
    scatter = (
        lax.broadcasted_iota(jnp.int32, (cot_ref.shape[0], voxels), 0) == target
    ).astype(bf16)
    partial_value = dot(hidden[...], wd_ref[...]).astype(bf16)
    coarse_ref[...] = dot(scatter, partial_value).astype(bf16)
    picked = dot(scatter, cot_ref[...], ((0,), (0,))).astype(bf16)
    dchildren = dot(picked, wd_ref[...], ((1,), (1,)))
    grad_down[...] = dot(hidden[...], picked, ((0,), (0,)))
    pairs[...] = jnp.zeros_like(pairs)
    for b in range(blocks):
        for c in range(8):
            rows = slice(b * voxels + c * 16, b * voxels + (c + 1) * 16)
            part = dchildren[b * 16:(b + 1) * 16, c * channels:(c + 1) * channels]
            dpre[rows, :] = (part * factor[rows, :]).astype(bf16)
        half = (b % 2) * voxels
        pairs[b // 2, half:half + voxels, half:half + voxels] = dpre[lanes(b), :]

    def weight_grad(j, c):
        rows = pl.ds(pl.multiple_of(j * 3 * channels, channels), 3 * channels)
        grad_sub[rows, :] = dot(flat_g[rows, :], dpre[...])
        return c

    lax.fori_loop(0, offsets // 3, weight_grad, 0)

    chip_rows = offsets * channels // (ny * nz)
    own = chip_rows // 2

    def stage(yy, c):
        first = pl.multiple_of(yy * nz * chip_rows, 16)
        slab = grad_sub[pl.ds(first, nz * chip_rows), :]
        down = grad_down[pl.ds(pl.multiple_of(yy * channels, channels), channels), :]
        for zz in range(nz):
            for cc in range(2):
                start = (zz * 2 + cc) * own
                parts[cc, 0, yy, zz] = slab[start:start + HALF_T * TILE_ROWS]
                rest = own - HALF_T * TILE_ROWS
                last = slab[start + HALF_T * TILE_ROWS:start + own]
                parts[cc, 1, zz, yy, 0:TILE_ROWS, :] = jnp.concatenate(
                    [last, jnp.zeros((TILE_ROWS - rest, channels), f32)], axis=0
                )
                start = (zz * 2 + cc) * TILE_ROWS
                for i in range(2):
                    rows = slice((i + 1) * TILE_ROWS, (i + 2) * TILE_ROWS)
                    parts[cc, 1, zz, yy, rows, :] = down[
                        start:start + TILE_ROWS, i * 128:(i + 1) * 128
                    ]
        return c

    lax.fori_loop(0, ny, stage, 0)

    step0 = []
    for h in range(2):
        def cast_half(i, c, h=h):
            send0[h, i] = parts[other, h, i].astype(bf16)
            return c
        lax.fori_loop(0, ny, cast_half, 0)
        step0.append(
            send(send0.at[h], recv0.at[h], ss0.at[h], rs0.at[h], place(y, z, other), x)
        )

    def spread(j, c):
        rows = pl.ds(pl.multiple_of(j * 3 * voxels, voxels), 3 * voxels)
        for p in range(blocks // 2):
            cols = pl.ds(p * 2 * voxels, 2 * voxels)
            both = dot(flat_p[rows, cols], pairs[p]).astype(bf16)
            for q in range(3):
                for i in range(2):
                    spread_v[(j * 3 + q) * blocks + 2 * p + i] = both[
                        q * voxels:(q + 1) * voxels, i * channels:(i + 1) * channels
                    ]
        return c

    lax.fori_loop(0, offsets // 3, spread, 0)

    step1 = []
    for h in range(2):
        step0[h].wait_recv()

        def add_core(i, c, h=h):
            total = parts[core, h, i] + recv0[h, i].astype(f32)
            acc1[h, i] = total
            send1[h, i] = total.astype(bf16)
            return c

        lax.fori_loop(0, ny, add_core, 0)
        for d in range(ny - 1):
            to = y_peers[d] if h == 0 else z_peers[d]
            t = place(to, z, core) if h == 0 else place(y, to, core)
            step1.append(send(send1.at[h, to], recv1.at[h, d], ss1.at[h, d], rs1.at[h, d], t, x))

    sort_copy.wait()

    def term(i, running):
        running = running * sort_s[2, i].astype(f32)
        running = running + dot(spread_v[sort_s[0, i]], ws_k[sort_s[1, i]])
        seg[i] = running
        return running

    lax.fori_loop(
        0, offsets * blocks, term, jnp.zeros((voxels, channels), f32), unroll=4
    )

    def block_grad(e):
        return seg[sort_s[3, e]] * sort_s[4, e].astype(f32)

    for i in range(FACE):
        out_h[0, i] = block_grad(i).astype(bf16)
        out_h[1, i] = block_grad(FACE + blocks + i).astype(bf16)
    returns = [
        send(out_h.at[0], in_h.at[1], ssg.at[0], rsg.at[0], before, x),
        send(out_h.at[1], in_h.at[0], ssg.at[1], rsg.at[1], after, x),
    ]

    step2 = []
    for h in range(2):
        for copy in step1[h * (ny - 1):(h + 1) * (ny - 1)]:
            copy.wait_recv()
        mine = y if h == 0 else z

        def add_axis(i, c, h=h, mine=mine):
            total = acc1[h, mine, i]
            for d in range(ny - 1):
                total = total + recv1[h, d, i].astype(f32)
            acc2[h, i] = total
            return c

        lax.fori_loop(0, nz, add_axis, 0)
        for d in range(nz - 1):
            to = z_peers[d] if h == 0 else y_peers[d]
            t = place(y, to, core) if h == 0 else place(to, z, core)
            step2.append(send(acc2.at[h, to], recv2.at[h, d], ss2.at[h, d], rs2.at[h, d], t, x))

    for copy in returns:
        copy.wait_recv()
    keep_u = mask_ref[...].astype(f32)
    for b in range(blocks):
        total = block_grad(FACE + b)
        if b < FACE:
            total = total + in_h[0, b].astype(f32)
        if b >= blocks - FACE:
            total = total + in_h[1, b - (blocks - FACE)].astype(f32)
        column = jnp.broadcast_to(keep_u[b:b + 1], total.shape).T
        grad_ref[b] = (column * total).astype(bf16)

    for h in range(2):
        for copy in step2[h * (nz - 1):(h + 1) * (nz - 1)]:
            copy.wait_recv()
        total = acc2[h, z if h == 0 else y]
        for d in range(nz - 1):
            total = total + recv2[h, d]
        share[h] = total
    recv3[x] = share[...]
    step3 = [
        send(share, recv3.at[x], ss3.at[d], rs3.at[d], tile, xx) for d, xx in enumerate(x_peers)
    ]
    for copy in step3:
        copy.wait_recv()
    total = recv3[0]
    for i in range(1, nx):
        total = total + recv3[i]
    total = total * scale
    half = HALF_T * TILE_ROWS
    sub_ref[0:half, :] = total[0]
    sub_ref[half:own, :] = total[1, 0:own - half]
    down_ref[:, 0:128] = total[1, TILE_ROWS:2 * TILE_ROWS]
    down_ref[:, 128:256] = total[1, 2 * TILE_ROWS:3 * TILE_ROWS]
    for copy in copies:
        copy.wait_send()


def on_device(
    features,
    w_sub,
    w_down,
    cotangent,
    vox_mask,
    nbr_owner,
    nbr_slot,
    voxel_map,
    parent_slot,
    parent_octant,
):
    _, blocks, voxels, channels = features.shape
    offsets = w_sub.shape[0]
    coarse_channels = w_down.shape[2]
    nx, tiles = lax.axis_size("dp"), lax.axis_size("tile")
    ny = 8
    nz = tiles // (2 * ny)
    f32, bf16, i32 = jnp.float32, jnp.bfloat16, jnp.int32
    tile_index = lax.axis_index("tile")
    owner, slot = nbr_owner[0], nbr_slot[0]
    present = owner >= 0
    position = jnp.where(present, (owner - tile_index) * blocks + FACE + slot, 0)
    octant = parent_octant[0]
    corner = (
        parent_slot[0] * voxels + 64 * (octant // 4) + 8 * ((octant // 2) % 2) + 2 * (octant % 2)
    )
    table = jnp.concatenate([
        position,
        jnp.where(present, 0, NO_VOXEL),
        jnp.pad(corner, (0, offsets - blocks))[None],
    ])
    entry = jnp.pad(
        position.T.reshape(1, -1), ((0, 0), (0, 256 - offsets * blocks)),
        constant_values=NO_BLOCK,
    )
    scale = float(nx * tiles * blocks * voxels) ** (-0.5)
    wide = blocks * voxels
    ext = blocks + 2 * FACE
    rows = HALF_T * TILE_ROWS
    own_rows = offsets * channels // tiles
    vmem = pl.BlockSpec(memory_space=pltpu.VMEM)
    smem = pl.BlockSpec(memory_space=pltpu.SMEM)
    dma = pltpu.SemaphoreType.DMA
    coarse_rows = cotangent.shape[1] * cotangent.shape[2]
    coarse, grad, sub, down = pl.pallas_call(
        functools.partial(kernel, (nx, ny, nz), scale),
        out_shape=(
            jax.ShapeDtypeStruct((coarse_rows, coarse_channels), bf16),
            jax.ShapeDtypeStruct((blocks, voxels, channels), bf16),
            jax.ShapeDtypeStruct((own_rows, channels), f32),
            jax.ShapeDtypeStruct((TILE_ROWS, coarse_channels), f32),
        ),
        in_specs=[smem] + [vmem] * 7,
        out_specs=(vmem,) * 4,
        scratch_shapes=[
            pltpu.VMEM((offsets, voxels, wide), bf16),
            pltpu.VMEM((offsets, channels, wide), bf16),
            pltpu.VMEM((ext, channels, voxels), bf16),
            pltpu.VMEM((2, FACE, channels, voxels), bf16),
            pltpu.VMEM((channels, offsets * channels), bf16),
            pltpu.VMEM((offsets, channels, channels), bf16),
            pltpu.VMEM((offsets * blocks, voxels, channels), bf16),
            pltpu.VMEM((blocks, PITCH, voxels), f32),
            pltpu.VMEM((channels, wide), f32),
            pltpu.VMEM((wide // 8, 8 * channels), bf16),
            pltpu.VMEM((wide, channels), f32),
            pltpu.VMEM((wide, channels), bf16),
            pltpu.VMEM((blocks // 2, 2 * voxels, 2 * channels), bf16),
            pltpu.VMEM((offsets * channels, channels), f32),
            pltpu.VMEM((8 * channels, coarse_channels), f32),
            pltpu.VMEM((TILE_ROWS, 256), i32),
            pltpu.SMEM((TILE_ROWS, 256), i32),
            pltpu.VMEM((offsets * blocks, voxels, channels), f32),
            pltpu.VMEM((2, 2, ny, nz, rows, 128), f32),
            pltpu.VMEM((2, ny, nz, rows, 128), bf16),
            pltpu.VMEM((2, ny, nz, rows, 128), bf16),
            pltpu.VMEM((2, ny, nz, rows, 128), f32),
            pltpu.VMEM((2, ny, nz, rows, 128), bf16),
            pltpu.VMEM((2, ny - 1, nz, rows, 128), bf16),
            pltpu.VMEM((2, nz, rows, 128), f32),
            pltpu.VMEM((2, nz - 1, rows, 128), f32),
            pltpu.VMEM((nx, 2, rows, 128), f32),
            pltpu.VMEM((2, rows, 128), f32),
            pltpu.VMEM((2, FACE, voxels, channels), bf16),
            pltpu.VMEM((2, FACE, voxels, channels), bf16),
            dma,
            dma((2,)), dma((2,)),
            dma((2, ny - 1)), dma((2, ny - 1)),
            dma((2, nz - 1)), dma((2, nz - 1)),
            dma((nx - 1,)), dma((nx - 1,)),
            dma((2,)), dma((2,)),
            dma((2,)), dma((2,)),
        ],
        compiler_params=pltpu.CompilerParams(
            collective_id=0, has_side_effects=True, vmem_limit_bytes=60 * 1024 * 1024
        ),
    )(
        table, entry, features[0], voxel_map[0], w_sub,
        w_down.reshape(-1, coarse_channels), cotangent[0].reshape(-1, coarse_channels),
        vox_mask[0],
    )
    return (
        coarse.reshape(cotangent.shape), grad[None], sub.reshape(-1), down.reshape(-1),
    )


def solution(mesh):
    in_specs = (
        P("dp", "tile", None, None),
        P(),
        P(),
        P("dp", "tile", None, None),
        P("dp", "tile", None),
        P("dp", "tile", None),
        P("dp", "tile", None),
        P("dp", "tile", None, None),
        P("dp", "tile"),
        P("dp", "tile"),
    )
    out_specs = (P("dp", "tile", None, None), P("dp", "tile", None, None), P("tile"), P("tile"))
    return jax.shard_map(
        on_device, mesh=mesh, in_specs=in_specs, out_specs=out_specs, check_vma=False
    )
```

```python
import functools

import jax
import jax.numpy as jnp
from jax import lax
from jax.experimental import pallas as pl
from jax.experimental.pallas import tpu as pltpu
from jax.sharding import PartitionSpec as P

FACE = 2
MESH = pl.DeviceIdType.MESH
TILE_ROWS = 8
HALF_T = 3
NO_BLOCK = 99
NO_VOXEL = 1000


def child_order(shape):
    new = lax.broadcasted_iota(jnp.int32, shape, 1)
    child, place = new // 16, new % 16
    z = 2 * (place // 4) + child // 4
    y = 2 * ((place // 2) % 2) + (child // 2) % 2
    x = 2 * (place % 2) + child % 2
    return 16 * z + 4 * y + x


def dot(a, b, dims=((1,), (0,))):
    return lax.dot_general(a, b, (dims, ((), ())), preferred_element_type=jnp.float32)


def sort_rows(e_row, count):
    wide = e_row.shape[1]
    square = (wide, wide)
    down = lax.broadcasted_iota(jnp.int32, square, 0)
    along = lax.broadcasted_iota(jnp.int32, square, 1)
    theirs = jnp.broadcast_to(e_row, square)
    mine = theirs.T

    def total(where, value=1):
        return jnp.sum(jnp.where(where, value, 0), axis=0, keepdims=True)

    rank = total((mine < theirs) | ((mine == theirs) & (down < along)))
    rank_down = jnp.broadcast_to(rank, square).T
    order = jnp.minimum(total(rank_down == along, down), count - 1)
    same = jnp.where(
        total(rank_down == along, mine) == total(rank_down == along - 1, mine), 1, 0
    )
    last = jnp.clip(total(mine <= along) - 1, 0, count - 1)
    some = jnp.minimum(total(mine == along), 1)
    return order, order // TILE_ROWS, same, last, some


def kernel(
    sizes, scale, table_ref, erow_ref, feat_ref, map_ref, ws_ref, wd_ref, cot_ref,
    mask_ref, coarse_ref, grad_ref, sub_ref, down_ref,
    picks, gathered, ext_t, halo_in, ws_t, ws_k, spread_v, map_p, pre_t, hidden, factor, dpre, pairs,
    grad_sub, grad_down, sort_v, sort_s, seg, parts,
    send0, recv0, acc1, send1, recv1, acc2, recv2, recv3, share, out_h, in_h,
    sort_sem, ss0, rs0, ss1, rs1, ss2, rs2, ss3, rs3, ssh, rsh, ssg, rsg,
):
    f32, bf16 = jnp.float32, jnp.bfloat16
    nx, ny, nz = sizes
    tile = lax.axis_index("tile")
    x = lax.axis_index("dp")
    core = lax.rem(tile, 2)
    z = lax.rem(tile // 2, nz)
    y = tile // (2 * nz)
    other = 1 - core
    count = 2 * ny * nz

    def place(yy, zz, cc):
        return (yy * nz + zz) * 2 + cc

    x_peers = [lax.rem(x + d, nx) for d in range(1, nx)]
    y_peers = [lax.rem(y + d, ny) for d in range(1, ny)]
    z_peers = [lax.rem(z + d, nz) for d in range(1, nz)]
    after, before = lax.rem(tile + 1, count), lax.rem(tile + count - 1, count)

    barrier = pltpu.get_barrier_semaphore()
    peers = [(place(y, z, other), x), (after, x), (before, x)]
    peers += [(tile, xx) for xx in x_peers]
    peers += [(place(yy, z, core), x) for yy in y_peers]
    peers += [(place(y, zz, core), x) for zz in z_peers]
    for peer in peers:
        pl.semaphore_signal(barrier, inc=1, device_id=peer, device_id_type=MESH)

    copies = []

    def send(src, dst, ss, rs, t, xx):
        copy = pltpu.make_async_remote_copy(
            src_ref=src, dst_ref=dst, send_sem=ss, recv_sem=rs,
            device_id=(t, xx), device_id_type=MESH,
        )
        copy.start()
        copies.append(copy)
        return copy

    offsets, voxels, wide = picks.shape
    blocks = wide // voxels
    channels = ws_ref.shape[1]
    lanes = lambda b: pl.ds(b * voxels, voxels)

    masks = mask_ref[...].astype(bf16)
    for b in range(blocks):
        ext_t[FACE + b] = feat_ref[b].T * masks[b:b + 1]
    pl.semaphore_wait(barrier, len(peers))
    halo = [
        send(ext_t.at[pl.ds(FACE, FACE)], halo_in.at[1], ssh.at[0], rsh.at[0], before, x),
        send(ext_t.at[pl.ds(blocks, FACE)], halo_in.at[0], ssh.at[1], rsh.at[1], after, x),
    ]
    sort_v[...] = jnp.zeros_like(sort_v)
    for i, row in enumerate(sort_rows(erow_ref[...], offsets * blocks)):
        sort_v[i:i + 1, :] = row
    sort_copy = pltpu.make_async_copy(sort_v, sort_s, sort_sem)
    sort_copy.start()

    perm = (
        lax.broadcasted_iota(jnp.int32, (voxels, voxels), 0) == child_order((voxels, voxels))
    ).astype(bf16)
    map_p[...] = dot(map_ref[...].astype(bf16), perm)
    keep = dot(masks, perm)
    row_ids = lax.broadcasted_iota(jnp.int32, (voxels, voxels), 0).astype(f32)

    def transpose_weight(k, c):
        weight = ws_ref[k].T
        ws_k[k] = weight
        ws_t[:, pl.ds(pl.multiple_of(k * channels, channels), channels)] = weight
        return c

    def gather(some, weights):
        def body(k, c):
            if weights:
                transpose_weight(k, c)
            maps = map_p[pl.ds(pl.multiple_of(k * blocks, blocks), blocks), :]
            for b in some:
                row = maps[b:b + 1] - table_ref[blocks + b, k].astype(f32)
                tile_bk = (row_ids == row).astype(bf16)
                picks[k, :, lanes(b)] = tile_bk
                gathered[k, :, lanes(b)] = dot(ext_t[table_ref[b, k]], tile_bk).astype(bf16)
            return c
        lax.fori_loop(0, offsets, body, 0, unroll=3)

    gather(range(FACE, blocks - FACE), True)
    for copy in halo:
        copy.wait_recv()
    for i in range(FACE):
        ext_t[i] = halo_in[0, i]
        ext_t[FACE + blocks + i] = halo_in[1, i]
    gather(list(range(FACE)) + list(range(blocks - FACE, blocks)), False)

    flat_g = gathered.reshape(offsets * channels, wide)
    flat_p = picks.reshape(offsets * voxels, wide)
    for p in range(blocks // 2):
        cols = pl.ds(p * 2 * voxels, 2 * voxels)
        pre_t[:, cols] = dot(ws_t[...], flat_g[:, cols])
    for b in range(blocks):
        pre = pre_t[:, lanes(b)]
        sig = jax.nn.sigmoid(pre)
        keep_b = keep[b:b + 1]
        hid = (keep_b * (pre * sig)).T.astype(bf16)
        for c in range(8):
            hidden[b * 16:(b + 1) * 16, c * channels:(c + 1) * channels] = hid[c * 16:(c + 1) * 16]
        factor[lanes(b), :] = (keep_b * sig * (1.0 + pre * (1.0 - sig))).T

    lane = lax.broadcasted_iota(jnp.int32, (1, voxels), 1)
    spot = lane % 16
    target = 16 * (spot // 4) + 4 * ((spot // 2) % 2) + spot % 2
    for b in range(blocks):
        target = target + jnp.where(lane // 16 == b, table_ref[2 * blocks, b], 0)
    scatter = (
        lax.broadcasted_iota(jnp.int32, (cot_ref.shape[0], voxels), 0) == target
    ).astype(bf16)
    partial_value = dot(hidden[...], wd_ref[...]).astype(bf16)
    coarse_ref[...] = dot(scatter, partial_value).astype(bf16)
    picked = dot(scatter, cot_ref[...], ((0,), (0,))).astype(bf16)
    dchildren = dot(picked, wd_ref[...], ((1,), (1,)))
    grad_down[...] = dot(hidden[...], picked, ((0,), (0,)))
    pairs[...] = jnp.zeros_like(pairs)
    for b in range(blocks):
        for c in range(8):
            rows = slice(b * voxels + c * 16, b * voxels + (c + 1) * 16)
            part = dchildren[b * 16:(b + 1) * 16, c * channels:(c + 1) * channels]
            dpre[rows, :] = (part * factor[rows, :]).astype(bf16)
        half = (b % 2) * voxels
        pairs[b // 2, half:half + voxels, half:half + voxels] = dpre[lanes(b), :]

    def weight_grad(j, c):
        rows = pl.ds(pl.multiple_of(j * 3 * channels, channels), 3 * channels)
        grad_sub[rows, :] = dot(flat_g[rows, :], dpre[...])
        return c

    lax.fori_loop(0, offsets // 3, weight_grad, 0)

    chip_rows = offsets * channels // (ny * nz)
    own = chip_rows // 2

    full = HALF_T * TILE_ROWS

    def stage_first(yy, c):
        first = pl.multiple_of(yy * nz * chip_rows, 16)
        slab = grad_sub[pl.ds(first, nz * chip_rows), :]
        for zz in range(nz):
            for cc in range(2):
                start = (zz * 2 + cc) * own
                parts[cc, 0, yy, zz] = slab[start:start + full]
        send0[0, yy] = parts[other, 0, yy].astype(bf16)
        return c

    def stage_second(yy, c):
        first = pl.multiple_of(yy * nz * chip_rows, 16)
        slab = grad_sub[pl.ds(first, nz * chip_rows), :]
        down = grad_down[pl.ds(pl.multiple_of(yy * channels, channels), channels), :]
        for zz in range(nz):
            for cc in range(2):
                start = (zz * 2 + cc) * own
                parts[cc, 1, zz, yy, 0:TILE_ROWS, :] = jnp.concatenate(
                    [slab[start + full:start + own], jnp.zeros((TILE_ROWS - own + full, channels), f32)],
                    axis=0,
                )
                start = (zz * 2 + cc) * TILE_ROWS
                for i in range(2):
                    rows = slice((i + 1) * TILE_ROWS, (i + 2) * TILE_ROWS)
                    parts[cc, 1, zz, yy, rows, :] = down[
                        start:start + TILE_ROWS, i * 128:(i + 1) * 128
                    ]
        return c

    def cast_second(i, c):
        send0[1, i] = parts[other, 1, i].astype(bf16)
        return c

    def send_half(h):
        return send(send0.at[h], recv0.at[h], ss0.at[h], rs0.at[h], place(y, z, other), x)

    lax.fori_loop(0, ny, stage_first, 0)
    step0 = [send_half(0)]
    lax.fori_loop(0, ny, stage_second, 0)
    lax.fori_loop(0, nz, cast_second, 0)
    step0.append(send_half(1))

    def spread(j, c):
        rows = pl.ds(pl.multiple_of(j * 3 * voxels, voxels), 3 * voxels)
        for p in range(blocks // 2):
            cols = pl.ds(p * 2 * voxels, 2 * voxels)
            both = dot(flat_p[rows, cols], pairs[p]).astype(bf16)
            for q in range(3):
                for i in range(2):
                    spread_v[(j * 3 + q) * blocks + 2 * p + i] = both[
                        q * voxels:(q + 1) * voxels, i * channels:(i + 1) * channels
                    ]
        return c

    early = offsets // 9
    lax.fori_loop(0, early, spread, 0)

    step1 = []
    for h in range(2):
        step0[h].wait_recv()

        def add_core(i, c, h=h):
            total = parts[core, h, i] + recv0[h, i].astype(f32)
            acc1[h, i] = total
            send1[h, i] = total.astype(bf16)
            return c

        lax.fori_loop(0, ny, add_core, 0)
        for d in range(ny - 1):
            to = y_peers[d] if h == 0 else z_peers[d]
            t = place(to, z, core) if h == 0 else place(y, to, core)
            step1.append(send(send1.at[h, to], recv1.at[h, d], ss1.at[h, d], rs1.at[h, d], t, x))

    lax.fori_loop(early, offsets // 3, spread, 0)
    sort_copy.wait()

    def term(i, running):
        running = running * sort_s[2, i].astype(f32)
        running = running + dot(spread_v[sort_s[0, i]], ws_k[sort_s[1, i]])
        seg[i] = running
        return running

    lax.fori_loop(
        0, offsets * blocks, term, jnp.zeros((voxels, channels), f32), unroll=4
    )

    def block_grad(e):
        return seg[sort_s[3, e]] * sort_s[4, e].astype(f32)

    for i in range(FACE):
        out_h[0, i] = block_grad(i).astype(bf16)
        out_h[1, i] = block_grad(FACE + blocks + i).astype(bf16)
    returns = [
        send(out_h.at[0], in_h.at[1], ssg.at[0], rsg.at[0], before, x),
        send(out_h.at[1], in_h.at[0], ssg.at[1], rsg.at[1], after, x),
    ]

    step2 = []
    for h in range(2):
        for copy in step1[h * (ny - 1):(h + 1) * (ny - 1)]:
            copy.wait_recv()
        mine = y if h == 0 else z

        def add_axis(i, c, h=h, mine=mine):
            total = acc1[h, mine, i]
            for d in range(ny - 1):
                total = total + recv1[h, d, i].astype(f32)
            acc2[h, i] = total
            return c

        lax.fori_loop(0, nz, add_axis, 0)
        for d in range(nz - 1):
            to = z_peers[d] if h == 0 else y_peers[d]
            t = place(y, to, core) if h == 0 else place(to, z, core)
            step2.append(send(acc2.at[h, to], recv2.at[h, d], ss2.at[h, d], rs2.at[h, d], t, x))

    for copy in returns:
        copy.wait_recv()
    keep_u = mask_ref[...].astype(f32)
    for b in range(blocks):
        total = block_grad(FACE + b)
        if b < FACE:
            total = total + in_h[0, b].astype(f32)
        if b >= blocks - FACE:
            total = total + in_h[1, b - (blocks - FACE)].astype(f32)
        column = jnp.broadcast_to(keep_u[b:b + 1], total.shape).T
        grad_ref[b] = (column * total).astype(bf16)

    for h in range(2):
        for copy in step2[h * (nz - 1):(h + 1) * (nz - 1)]:
            copy.wait_recv()
        total = acc2[h, z if h == 0 else y]
        for d in range(nz - 1):
            total = total + recv2[h, d]
        share[h] = total
    recv3[x] = share[...]
    step3 = [
        send(share, recv3.at[x], ss3.at[d], rs3.at[d], tile, xx) for d, xx in enumerate(x_peers)
    ]
    for copy in step3:
        copy.wait_recv()
    total = recv3[0]
    for i in range(1, nx):
        total = total + recv3[i]
    total = total * scale
    half = HALF_T * TILE_ROWS
    sub_ref[0:half, :] = total[0]
    sub_ref[half:own, :] = total[1, 0:own - half]
    for i in range(2):
        down_ref[pl.ds(i, TILE_ROWS, 2), :] = total[1, (i + 1) * TILE_ROWS:(i + 2) * TILE_ROWS]
    for copy in copies:
        copy.wait_send()


def finish_kernel(*refs):
    arrays = len(refs) // 2
    for source, result in zip(refs[:arrays], refs[arrays:]):
        result[...] = source[...]


def finish(*arrays):
    vmem = pl.BlockSpec(memory_space=pltpu.VMEM)
    return pl.pallas_call(
        finish_kernel,
        out_shape=tuple(jax.ShapeDtypeStruct(a.shape, a.dtype) for a in arrays),
        in_specs=[vmem] * len(arrays),
        out_specs=(vmem,) * len(arrays),
    )(*arrays)


def on_device(
    features,
    w_sub,
    w_down,
    cotangent,
    vox_mask,
    nbr_owner,
    nbr_slot,
    voxel_map,
    parent_slot,
    parent_octant,
):
    _, blocks, voxels, channels = features.shape
    offsets = w_sub.shape[0]
    coarse_channels = w_down.shape[2]
    nx, tiles = lax.axis_size("dp"), lax.axis_size("tile")
    ny = 8
    nz = tiles // (2 * ny)
    f32, bf16, i32 = jnp.float32, jnp.bfloat16, jnp.int32
    tile_index = lax.axis_index("tile")
    owner, slot = nbr_owner[0], nbr_slot[0]
    present = owner >= 0
    position = jnp.where(present, (owner - tile_index) * blocks + FACE + slot, 0)
    octant = parent_octant[0]
    corner = (
        parent_slot[0] * voxels + 64 * (octant // 4) + 8 * ((octant // 2) % 2) + 2 * (octant % 2)
    )
    table = jnp.concatenate([
        position,
        jnp.where(present, 0, NO_VOXEL),
        jnp.pad(corner, (0, offsets - blocks))[None],
    ])
    maps = jnp.transpose(voxel_map[0], (1, 0, 2)).reshape(-1, voxels)
    entry = jnp.pad(
        position.T.reshape(1, -1), ((0, 0), (0, 256 - offsets * blocks)),
        constant_values=NO_BLOCK,
    )
    scale = float(nx * tiles * blocks * voxels) ** (-0.5)
    wide = blocks * voxels
    ext = blocks + 2 * FACE
    rows = HALF_T * TILE_ROWS
    own_rows = offsets * channels // tiles
    vmem = pl.BlockSpec(memory_space=pltpu.VMEM)
    smem = pl.BlockSpec(memory_space=pltpu.SMEM)
    dma = pltpu.SemaphoreType.DMA
    coarse_rows = cotangent.shape[1] * cotangent.shape[2]
    coarse, grad, sub, down = pl.pallas_call(
        functools.partial(kernel, (nx, ny, nz), scale),
        out_shape=(
            jax.ShapeDtypeStruct((coarse_rows, coarse_channels), bf16),
            jax.ShapeDtypeStruct((blocks, voxels, channels), bf16),
            jax.ShapeDtypeStruct((own_rows, channels), f32),
            jax.ShapeDtypeStruct((2 * TILE_ROWS, channels), f32),
        ),
        in_specs=[smem] + [vmem] * 7,
        out_specs=(vmem,) * 4,
        scratch_shapes=[
            pltpu.VMEM((offsets, voxels, wide), bf16),
            pltpu.VMEM((offsets, channels, wide), bf16),
            pltpu.VMEM((ext, channels, voxels), bf16),
            pltpu.VMEM((2, FACE, channels, voxels), bf16),
            pltpu.VMEM((channels, offsets * channels), bf16),
            pltpu.VMEM((offsets, channels, channels), bf16),
            pltpu.VMEM((offsets * blocks, voxels, channels), bf16),
            pltpu.VMEM((offsets * blocks, voxels), f32),
            pltpu.VMEM((channels, wide), f32),
            pltpu.VMEM((wide // 8, 8 * channels), bf16),
            pltpu.VMEM((wide, channels), f32),
            pltpu.VMEM((wide, channels), bf16),
            pltpu.VMEM((blocks // 2, 2 * voxels, 2 * channels), bf16),
            pltpu.VMEM((offsets * channels, channels), f32),
            pltpu.VMEM((8 * channels, coarse_channels), f32),
            pltpu.VMEM((TILE_ROWS, 256), i32),
            pltpu.SMEM((TILE_ROWS, 256), i32),
            pltpu.VMEM((offsets * blocks, voxels, channels), f32),
            pltpu.VMEM((2, 2, ny, nz, rows, 128), f32),
            pltpu.VMEM((2, ny, nz, rows, 128), bf16),
            pltpu.VMEM((2, ny, nz, rows, 128), bf16),
            pltpu.VMEM((2, ny, nz, rows, 128), f32),
            pltpu.VMEM((2, ny, nz, rows, 128), bf16),
            pltpu.VMEM((2, ny - 1, nz, rows, 128), bf16),
            pltpu.VMEM((2, nz, rows, 128), f32),
            pltpu.VMEM((2, nz - 1, rows, 128), f32),
            pltpu.VMEM((nx, 2, rows, 128), f32),
            pltpu.VMEM((2, rows, 128), f32),
            pltpu.VMEM((2, FACE, voxels, channels), bf16),
            pltpu.VMEM((2, FACE, voxels, channels), bf16),
            dma,
            dma((2,)), dma((2,)),
            dma((2, ny - 1)), dma((2, ny - 1)),
            dma((2, nz - 1)), dma((2, nz - 1)),
            dma((nx - 1,)), dma((nx - 1,)),
            dma((2,)), dma((2,)),
            dma((2,)), dma((2,)),
        ],
        compiler_params=pltpu.CompilerParams(
            collective_id=0, has_side_effects=True, vmem_limit_bytes=60 * 1024 * 1024
        ),
    )(
        table, entry, features[0], maps, w_sub,
        w_down.reshape(-1, coarse_channels), cotangent[0].reshape(-1, coarse_channels),
        vox_mask[0],
    )
    coarse, grad, sub, down = finish(coarse, grad, sub, down)
    return (
        coarse.reshape(cotangent.shape), grad[None], sub.reshape(-1), down.reshape(-1),
    )


def solution(mesh):
    in_specs = (
        P("dp", "tile", None, None),
        P(),
        P(),
        P("dp", "tile", None, None),
        P("dp", "tile", None),
        P("dp", "tile", None),
        P("dp", "tile", None),
        P("dp", "tile", None, None),
        P("dp", "tile"),
        P("dp", "tile"),
    )
    out_specs = (P("dp", "tile", None, None), P("dp", "tile", None, None), P("tile"), P("tile"))
    return jax.shard_map(
        on_device, mesh=mesh, in_specs=in_specs, out_specs=out_specs, check_vma=False
    )
```

```python
import functools

import jax
import jax.numpy as jnp
from jax import lax
from jax.experimental import pallas as pl
from jax.experimental.pallas import tpu as pltpu
from jax.sharding import PartitionSpec as P

FACE = 2
MESH = pl.DeviceIdType.MESH
TILE_ROWS = 8
HALF_T = 3
NO_BLOCK = 99
NO_VOXEL = 1000


def child_order(shape):
    new = lax.broadcasted_iota(jnp.int32, shape, 1)
    child, place = new // 16, new % 16
    z = 2 * (place // 4) + child // 4
    y = 2 * ((place // 2) % 2) + (child // 2) % 2
    x = 2 * (place % 2) + child % 2
    return 16 * z + 4 * y + x


def dot(a, b, dims=((1,), (0,))):
    return lax.dot_general(a, b, (dims, ((), ())), preferred_element_type=jnp.float32)


def sort_rows(e_row, count):
    wide = e_row.shape[1]
    square = (wide, wide)
    down = lax.broadcasted_iota(jnp.int32, square, 0)
    along = lax.broadcasted_iota(jnp.int32, square, 1)
    theirs = jnp.broadcast_to(e_row, square)
    mine = theirs.T

    def total(where, value=1):
        return jnp.sum(jnp.where(where, value, 0), axis=0, keepdims=True)

    rank = total((mine < theirs) | ((mine == theirs) & (down < along)))
    rank_down = jnp.broadcast_to(rank, square).T
    order = jnp.minimum(total(rank_down == along, down), count - 1)
    same = jnp.where(
        total(rank_down == along, mine) == total(rank_down == along - 1, mine), 1, 0
    )
    last = jnp.clip(total(mine <= along) - 1, 0, count - 1)
    some = jnp.minimum(total(mine == along), 1)
    return order, order // TILE_ROWS, same, last, some


def kernel(
    sizes, scale, table_ref, erow_ref, feat_ref, map_ref, ws_ref, wd_ref, cot_ref,
    mask_ref, coarse_ref, grad_ref, sub_ref, down_ref,
    picks, gathered, ext_t, halo_in, ws_t, ws_k, spread_v, map_p, pre_t, hidden, factor, dpre, pairs,
    grad_sub, grad_down, sort_v, sort_s, seg, parts,
    send0, recv0, acc1, send1, recv1, acc2, recv2, recv3, share, out_h, in_h,
    sort_sem, ss0, rs0, ss1, rs1, ss2, rs2, ss3, rs3, ssh, rsh, ssg, rsg,
):
    f32, bf16 = jnp.float32, jnp.bfloat16
    nx, ny, nz = sizes
    tile = lax.axis_index("tile")
    x = lax.axis_index("dp")
    core = lax.rem(tile, 2)
    z = lax.rem(tile // 2, nz)
    y = tile // (2 * nz)
    other = 1 - core
    count = 2 * ny * nz

    def place(yy, zz, cc):
        return (yy * nz + zz) * 2 + cc

    x_peers = [lax.rem(x + d, nx) for d in range(1, nx)]
    y_peers = [lax.rem(y + d, ny) for d in range(1, ny)]
    z_peers = [lax.rem(z + d, nz) for d in range(1, nz)]
    after, before = lax.rem(tile + 1, count), lax.rem(tile + count - 1, count)

    barrier = pltpu.get_barrier_semaphore()
    peers = [(place(y, z, other), x), (after, x), (before, x)]
    peers += [(tile, xx) for xx in x_peers]
    peers += [(place(yy, z, core), x) for yy in y_peers]
    peers += [(place(y, zz, core), x) for zz in z_peers]
    for peer in peers:
        pl.semaphore_signal(barrier, inc=1, device_id=peer, device_id_type=MESH)

    copies = []

    def send(src, dst, ss, rs, t, xx):
        copy = pltpu.make_async_remote_copy(
            src_ref=src, dst_ref=dst, send_sem=ss, recv_sem=rs,
            device_id=(t, xx), device_id_type=MESH,
        )
        copy.start()
        copies.append(copy)
        return copy

    offsets, voxels, wide = picks.shape
    blocks = wide // voxels
    channels = ws_ref.shape[1]
    lanes = lambda b: pl.ds(b * voxels, voxels)

    masks = mask_ref[...].astype(bf16)
    for b in range(blocks):
        ext_t[FACE + b] = feat_ref[b].T * masks[b:b + 1]
    pl.semaphore_wait(barrier, len(peers))
    halo = [
        send(ext_t.at[pl.ds(FACE, FACE)], halo_in.at[1], ssh.at[0], rsh.at[0], before, x),
        send(ext_t.at[pl.ds(blocks, FACE)], halo_in.at[0], ssh.at[1], rsh.at[1], after, x),
    ]
    sort_v[...] = jnp.zeros_like(sort_v)
    for i, row in enumerate(sort_rows(erow_ref[...], offsets * blocks)):
        sort_v[i:i + 1, :] = row
    sort_copy = pltpu.make_async_copy(sort_v, sort_s, sort_sem)
    sort_copy.start()

    perm = (
        lax.broadcasted_iota(jnp.int32, (voxels, voxels), 0) == child_order((voxels, voxels))
    ).astype(bf16)
    map_p[...] = dot(map_ref[...].astype(bf16), perm)
    keep = dot(masks, perm)
    row_ids = lax.broadcasted_iota(jnp.int32, (voxels, voxels), 0).astype(f32)

    def transpose_weight(k, c):
        weight = ws_ref[k].T
        ws_k[k] = weight
        ws_t[:, pl.ds(pl.multiple_of(k * channels, channels), channels)] = weight
        return c

    def gather(some, weights):
        def body(k, c):
            if weights:
                transpose_weight(k, c)
            maps = map_p[pl.ds(pl.multiple_of(k * blocks, blocks), blocks), :]
            for b in some:
                row = maps[b:b + 1] - table_ref[blocks + b, k].astype(f32)
                tile_bk = (row_ids == row).astype(bf16)
                picks[k, :, lanes(b)] = tile_bk
                gathered[k, :, lanes(b)] = dot(ext_t[table_ref[b, k]], tile_bk).astype(bf16)
            return c
        lax.fori_loop(0, offsets, body, 0, unroll=9)

    gather(range(FACE, blocks - FACE), True)
    for copy in halo:
        copy.wait_recv()
    for i in range(FACE):
        ext_t[i] = halo_in[0, i]
        ext_t[FACE + blocks + i] = halo_in[1, i]
    gather(list(range(FACE)) + list(range(blocks - FACE, blocks)), False)

    flat_g = gathered.reshape(offsets * channels, wide)
    flat_p = picks.reshape(offsets * voxels, wide)
    for p in range(blocks // 2):
        cols = pl.ds(p * 2 * voxels, 2 * voxels)
        pre_t[:, cols] = dot(ws_t[...], flat_g[:, cols])
    for b in range(blocks):
        pre = pre_t[:, lanes(b)]
        sig = jax.nn.sigmoid(pre)
        keep_b = keep[b:b + 1]
        hid = (keep_b * (pre * sig)).T.astype(bf16)
        for c in range(8):
            hidden[b * 16:(b + 1) * 16, c * channels:(c + 1) * channels] = hid[c * 16:(c + 1) * 16]
        factor[lanes(b), :] = (keep_b * sig * (1.0 + pre * (1.0 - sig))).T

    lane = lax.broadcasted_iota(jnp.int32, (1, voxels), 1)
    spot = lane % 16
    target = 16 * (spot // 4) + 4 * ((spot // 2) % 2) + spot % 2
    for b in range(blocks):
        target = target + jnp.where(lane // 16 == b, table_ref[2 * blocks, b], 0)
    scatter = (
        lax.broadcasted_iota(jnp.int32, (cot_ref.shape[0], voxels), 0) == target
    ).astype(bf16)
    partial_value = dot(hidden[...], wd_ref[...]).astype(bf16)
    coarse_ref[...] = dot(scatter, partial_value).astype(bf16)
    picked = dot(scatter, cot_ref[...], ((0,), (0,))).astype(bf16)
    dchildren = dot(picked, wd_ref[...], ((1,), (1,)))
    grad_down[...] = dot(hidden[...], picked, ((0,), (0,)))
    pairs[...] = jnp.zeros_like(pairs)
    for b in range(blocks):
        for c in range(8):
            rows = slice(b * voxels + c * 16, b * voxels + (c + 1) * 16)
            part = dchildren[b * 16:(b + 1) * 16, c * channels:(c + 1) * channels]
            dpre[rows, :] = (part * factor[rows, :]).astype(bf16)
        half = (b % 2) * voxels
        pairs[b // 2, half:half + voxels, half:half + voxels] = dpre[lanes(b), :]

    def weight_grad(j, c):
        rows = pl.ds(pl.multiple_of(j * 3 * channels, channels), 3 * channels)
        grad_sub[rows, :] = dot(flat_g[rows, :], dpre[...])
        return c

    lax.fori_loop(0, offsets // 3, weight_grad, 0, unroll=3)

    chip_rows = offsets * channels // (ny * nz)
    own = chip_rows // 2

    full = HALF_T * TILE_ROWS

    def stage_first(yy, c):
        first = pl.multiple_of(yy * nz * chip_rows, 16)
        slab = grad_sub[pl.ds(first, nz * chip_rows), :]
        for zz in range(nz):
            for cc in range(2):
                start = (zz * 2 + cc) * own
                parts[cc, 0, yy, zz] = slab[start:start + full]
        send0[0, yy] = parts[other, 0, yy].astype(bf16)
        return c

    def stage_second(yy, c):
        first = pl.multiple_of(yy * nz * chip_rows, 16)
        slab = grad_sub[pl.ds(first, nz * chip_rows), :]
        down = grad_down[pl.ds(pl.multiple_of(yy * channels, channels), channels), :]
        for zz in range(nz):
            for cc in range(2):
                start = (zz * 2 + cc) * own
                parts[cc, 1, zz, yy, 0:TILE_ROWS, :] = jnp.concatenate(
                    [slab[start + full:start + own], jnp.zeros((TILE_ROWS - own + full, channels), f32)],
                    axis=0,
                )
                start = (zz * 2 + cc) * TILE_ROWS
                for i in range(2):
                    rows = slice((i + 1) * TILE_ROWS, (i + 2) * TILE_ROWS)
                    parts[cc, 1, zz, yy, rows, :] = down[
                        start:start + TILE_ROWS, i * 128:(i + 1) * 128
                    ]
        return c

    def cast_second(i, c):
        send0[1, i] = parts[other, 1, i].astype(bf16)
        return c

    def send_half(h):
        return send(send0.at[h], recv0.at[h], ss0.at[h], rs0.at[h], place(y, z, other), x)

    lax.fori_loop(0, ny, stage_first, 0)
    step0 = [send_half(0)]
    lax.fori_loop(0, ny, stage_second, 0)
    lax.fori_loop(0, nz, cast_second, 0)
    step0.append(send_half(1))

    def spread(j, c):
        rows = pl.ds(pl.multiple_of(j * 3 * voxels, voxels), 3 * voxels)
        for p in range(blocks // 2):
            cols = pl.ds(p * 2 * voxels, 2 * voxels)
            both = dot(flat_p[rows, cols], pairs[p]).astype(bf16)
            for q in range(3):
                for i in range(2):
                    spread_v[(j * 3 + q) * blocks + 2 * p + i] = both[
                        q * voxels:(q + 1) * voxels, i * channels:(i + 1) * channels
                    ]
        return c

    early = offsets // 9
    lax.fori_loop(0, early, spread, 0)

    step1 = []
    for h in range(2):
        step0[h].wait_recv()

        def add_core(i, c, h=h):
            total = parts[core, h, i] + recv0[h, i].astype(f32)
            acc1[h, i] = total
            send1[h, i] = total.astype(bf16)
            return c

        lax.fori_loop(0, ny, add_core, 0)
        for d in range(ny - 1):
            to = y_peers[d] if h == 0 else z_peers[d]
            t = place(to, z, core) if h == 0 else place(y, to, core)
            step1.append(send(send1.at[h, to], recv1.at[h, d], ss1.at[h, d], rs1.at[h, d], t, x))

    lax.fori_loop(early, offsets // 3, spread, 0)
    sort_copy.wait()

    def term(i, running):
        running = running * sort_s[2, i].astype(f32)
        running = running + dot(spread_v[sort_s[0, i]], ws_k[sort_s[1, i]])
        seg[i] = running
        return running

    lax.fori_loop(
        0, offsets * blocks, term, jnp.zeros((voxels, channels), f32), unroll=8
    )

    def block_grad(e):
        return seg[sort_s[3, e]] * sort_s[4, e].astype(f32)

    for i in range(FACE):
        out_h[0, i] = block_grad(i).astype(bf16)
        out_h[1, i] = block_grad(FACE + blocks + i).astype(bf16)
    returns = [
        send(out_h.at[0], in_h.at[1], ssg.at[0], rsg.at[0], before, x),
        send(out_h.at[1], in_h.at[0], ssg.at[1], rsg.at[1], after, x),
    ]

    step2 = []
    for h in range(2):
        for copy in step1[h * (ny - 1):(h + 1) * (ny - 1)]:
            copy.wait_recv()
        mine = y if h == 0 else z

        def add_axis(i, c, h=h, mine=mine):
            total = acc1[h, mine, i]
            for d in range(ny - 1):
                total = total + recv1[h, d, i].astype(f32)
            acc2[h, i] = total
            return c

        lax.fori_loop(0, nz, add_axis, 0)
        for d in range(nz - 1):
            to = z_peers[d] if h == 0 else y_peers[d]
            t = place(y, to, core) if h == 0 else place(to, z, core)
            step2.append(send(acc2.at[h, to], recv2.at[h, d], ss2.at[h, d], rs2.at[h, d], t, x))

    for copy in returns:
        copy.wait_recv()
    keep_u = mask_ref[...].astype(f32)
    for b in range(blocks):
        total = block_grad(FACE + b)
        if b < FACE:
            total = total + in_h[0, b].astype(f32)
        if b >= blocks - FACE:
            total = total + in_h[1, b - (blocks - FACE)].astype(f32)
        column = jnp.broadcast_to(keep_u[b:b + 1], total.shape).T
        grad_ref[b] = (column * total).astype(bf16)

    for h in range(2):
        for copy in step2[h * (nz - 1):(h + 1) * (nz - 1)]:
            copy.wait_recv()
        total = acc2[h, z if h == 0 else y]
        for d in range(nz - 1):
            total = total + recv2[h, d]
        share[h] = total
    recv3[x] = share[...]
    step3 = [
        send(share, recv3.at[x], ss3.at[d], rs3.at[d], tile, xx) for d, xx in enumerate(x_peers)
    ]
    for copy in step3:
        copy.wait_recv()
    total = recv3[0]
    for i in range(1, nx):
        total = total + recv3[i]
    total = total * scale
    half = HALF_T * TILE_ROWS
    sub_ref[0:half, :] = total[0]
    sub_ref[half:own, :] = total[1, 0:own - half]
    for i in range(2):
        down_ref[pl.ds(i, TILE_ROWS, 2), :] = total[1, (i + 1) * TILE_ROWS:(i + 2) * TILE_ROWS]
    for copy in copies:
        copy.wait_send()


def finish_kernel(*refs):
    arrays = len(refs) // 2
    for source, result in zip(refs[:arrays], refs[arrays:]):
        result[...] = source[...]


def finish(*arrays):
    vmem = pl.BlockSpec(memory_space=pltpu.VMEM)
    return pl.pallas_call(
        finish_kernel,
        out_shape=tuple(jax.ShapeDtypeStruct(a.shape, a.dtype) for a in arrays),
        in_specs=[vmem] * len(arrays),
        out_specs=(vmem,) * len(arrays),
    )(*arrays)


def on_device(
    features,
    w_sub,
    w_down,
    cotangent,
    vox_mask,
    nbr_owner,
    nbr_slot,
    voxel_map,
    parent_slot,
    parent_octant,
):
    _, blocks, voxels, channels = features.shape
    offsets = w_sub.shape[0]
    coarse_channels = w_down.shape[2]
    nx, tiles = lax.axis_size("dp"), lax.axis_size("tile")
    ny = 8
    nz = tiles // (2 * ny)
    f32, bf16, i32 = jnp.float32, jnp.bfloat16, jnp.int32
    tile_index = lax.axis_index("tile")
    owner, slot = nbr_owner[0], nbr_slot[0]
    present = owner >= 0
    position = jnp.where(present, (owner - tile_index) * blocks + FACE + slot, 0)
    octant = parent_octant[0]
    corner = (
        parent_slot[0] * voxels + 64 * (octant // 4) + 8 * ((octant // 2) % 2) + 2 * (octant % 2)
    )
    table = jnp.concatenate([
        position,
        jnp.where(present, 0, NO_VOXEL),
        jnp.pad(corner, (0, offsets - blocks))[None],
    ])
    maps = jnp.transpose(voxel_map[0], (1, 0, 2)).reshape(-1, voxels)
    entry = jnp.pad(
        position.T.reshape(1, -1), ((0, 0), (0, 256 - offsets * blocks)),
        constant_values=NO_BLOCK,
    )
    scale = float(nx * tiles * blocks * voxels) ** (-0.5)
    wide = blocks * voxels
    ext = blocks + 2 * FACE
    rows = HALF_T * TILE_ROWS
    own_rows = offsets * channels // tiles
    vmem = pl.BlockSpec(memory_space=pltpu.VMEM)
    smem = pl.BlockSpec(memory_space=pltpu.SMEM)
    dma = pltpu.SemaphoreType.DMA
    coarse_rows = cotangent.shape[1] * cotangent.shape[2]
    coarse, grad, sub, down = pl.pallas_call(
        functools.partial(kernel, (nx, ny, nz), scale),
        out_shape=(
            jax.ShapeDtypeStruct((coarse_rows, coarse_channels), bf16),
            jax.ShapeDtypeStruct((blocks, voxels, channels), bf16),
            jax.ShapeDtypeStruct((own_rows, channels), f32),
            jax.ShapeDtypeStruct((2 * TILE_ROWS, channels), f32),
        ),
        in_specs=[smem] + [vmem] * 7,
        out_specs=(vmem,) * 4,
        scratch_shapes=[
            pltpu.VMEM((offsets, voxels, wide), bf16),
            pltpu.VMEM((offsets, channels, wide), bf16),
            pltpu.VMEM((ext, channels, voxels), bf16),
            pltpu.VMEM((2, FACE, channels, voxels), bf16),
            pltpu.VMEM((channels, offsets * channels), bf16),
            pltpu.VMEM((offsets, channels, channels), bf16),
            pltpu.VMEM((offsets * blocks, voxels, channels), bf16),
            pltpu.VMEM((offsets * blocks, voxels), f32),
            pltpu.VMEM((channels, wide), f32),
            pltpu.VMEM((wide // 8, 8 * channels), bf16),
            pltpu.VMEM((wide, channels), f32),
            pltpu.VMEM((wide, channels), bf16),
            pltpu.VMEM((blocks // 2, 2 * voxels, 2 * channels), bf16),
            pltpu.VMEM((offsets * channels, channels), f32),
            pltpu.VMEM((8 * channels, coarse_channels), f32),
            pltpu.VMEM((TILE_ROWS, 256), i32),
            pltpu.SMEM((TILE_ROWS, 256), i32),
            pltpu.VMEM((offsets * blocks, voxels, channels), f32),
            pltpu.VMEM((2, 2, ny, nz, rows, 128), f32),
            pltpu.VMEM((2, ny, nz, rows, 128), bf16),
            pltpu.VMEM((2, ny, nz, rows, 128), bf16),
            pltpu.VMEM((2, ny, nz, rows, 128), f32),
            pltpu.VMEM((2, ny, nz, rows, 128), bf16),
            pltpu.VMEM((2, ny - 1, nz, rows, 128), bf16),
            pltpu.VMEM((2, nz, rows, 128), f32),
            pltpu.VMEM((2, nz - 1, rows, 128), f32),
            pltpu.VMEM((nx, 2, rows, 128), f32),
            pltpu.VMEM((2, rows, 128), f32),
            pltpu.VMEM((2, FACE, voxels, channels), bf16),
            pltpu.VMEM((2, FACE, voxels, channels), bf16),
            dma,
            dma((2,)), dma((2,)),
            dma((2, ny - 1)), dma((2, ny - 1)),
            dma((2, nz - 1)), dma((2, nz - 1)),
            dma((nx - 1,)), dma((nx - 1,)),
            dma((2,)), dma((2,)),
            dma((2,)), dma((2,)),
        ],
        compiler_params=pltpu.CompilerParams(
            collective_id=0, has_side_effects=True, vmem_limit_bytes=60 * 1024 * 1024
        ),
    )(
        table, entry, features[0], maps, w_sub,
        w_down.reshape(-1, coarse_channels), cotangent[0].reshape(-1, coarse_channels),
        vox_mask[0],
    )
    coarse, grad, sub, down = finish(coarse, grad, sub, down)
    return (
        coarse.reshape(cotangent.shape), grad[None], sub.reshape(-1), down.reshape(-1),
    )


def solution(mesh):
    in_specs = (
        P("dp", "tile", None, None),
        P(),
        P(),
        P("dp", "tile", None, None),
        P("dp", "tile", None),
        P("dp", "tile", None),
        P("dp", "tile", None),
        P("dp", "tile", None, None),
        P("dp", "tile"),
        P("dp", "tile"),
    )
    out_specs = (P("dp", "tile", None, None), P("dp", "tile", None, None), P("tile"), P("tile"))
    return jax.shard_map(
        on_device, mesh=mesh, in_specs=in_specs, out_specs=out_specs, check_vma=False
    )
```

```python
import functools

import jax
import jax.numpy as jnp
from jax import lax
from jax.experimental import pallas as pl
from jax.experimental.pallas import tpu as pltpu
from jax.sharding import PartitionSpec as P

FACE = 2
MESH = pl.DeviceIdType.MESH
TILE_ROWS = 8
HALF_T = 3
NO_BLOCK = 99
NO_VOXEL = 1000


def child_order(shape):
    new = lax.broadcasted_iota(jnp.int32, shape, 1)
    child, place = new // 16, new % 16
    z = 2 * (place // 4) + child // 4
    y = 2 * ((place // 2) % 2) + (child // 2) % 2
    x = 2 * (place % 2) + child % 2
    return 16 * z + 4 * y + x


def dot(a, b, dims=((1,), (0,))):
    return lax.dot_general(a, b, (dims, ((), ())), preferred_element_type=jnp.float32)


def sort_rows(e_row, count):
    wide = e_row.shape[1]
    square = (wide, wide)
    down = lax.broadcasted_iota(jnp.int32, square, 0)
    along = lax.broadcasted_iota(jnp.int32, square, 1)
    theirs = jnp.broadcast_to(e_row, square)
    mine = theirs.T

    def total(where, value=1):
        return jnp.sum(jnp.where(where, value, 0), axis=0, keepdims=True)

    rank = total((mine < theirs) | ((mine == theirs) & (down < along)))
    rank_down = jnp.broadcast_to(rank, square).T
    order = jnp.minimum(total(rank_down == along, down), count - 1)
    same = jnp.where(
        total(rank_down == along, mine) == total(rank_down == along - 1, mine), 1, 0
    )
    last = jnp.clip(total(mine <= along) - 1, 0, count - 1)
    some = jnp.minimum(total(mine == along), 1)
    return order, order // TILE_ROWS, same, last, some


def kernel(
    sizes, scale, table_ref, erow_ref, feat_ref, map_ref, ws_ref, wd_ref, cot_ref,
    mask_ref, coarse_ref, grad_ref, sub_ref, down_ref,
    picks, gathered, ext_t, halo_in, ws_t, ws_k, spread_v, map_p, pre_t, hidden, factor, dpre, pairs,
    grad_sub, grad_down, sort_v, sort_s, seg, parts,
    send0, recv0, acc1, send1, recv1, acc2, recv2, recv3, share, out_h, in_h,
    sort_sem, ss0, rs0, ss1, rs1, ss2, rs2, ss3, rs3, ssh, rsh, ssg, rsg,
):
    f32, bf16 = jnp.float32, jnp.bfloat16
    nx, ny, nz = sizes
    tile = lax.axis_index("tile")
    x = lax.axis_index("dp")
    core = lax.rem(tile, 2)
    z = lax.rem(tile // 2, nz)
    y = tile // (2 * nz)
    other = 1 - core
    count = 2 * ny * nz

    def place(yy, zz, cc):
        return (yy * nz + zz) * 2 + cc

    x_peers = [lax.rem(x + d, nx) for d in range(1, nx)]
    y_peers = [lax.rem(y + d, ny) for d in range(1, ny)]
    z_peers = [lax.rem(z + d, nz) for d in range(1, nz)]
    after, before = lax.rem(tile + 1, count), lax.rem(tile + count - 1, count)

    barrier = pltpu.get_barrier_semaphore()
    peers = [(place(y, z, other), x), (after, x), (before, x)]
    peers += [(tile, xx) for xx in x_peers]
    peers += [(place(yy, z, core), x) for yy in y_peers]
    peers += [(place(y, zz, core), x) for zz in z_peers]
    for peer in peers:
        pl.semaphore_signal(barrier, inc=1, device_id=peer, device_id_type=MESH)

    copies = []

    def send(src, dst, ss, rs, t, xx):
        copy = pltpu.make_async_remote_copy(
            src_ref=src, dst_ref=dst, send_sem=ss, recv_sem=rs,
            device_id=(t, xx), device_id_type=MESH,
        )
        copy.start()
        copies.append(copy)
        return copy

    offsets, voxels, wide = picks.shape
    blocks = wide // voxels
    channels = ws_ref.shape[1]
    lanes = lambda b: pl.ds(b * voxels, voxels)

    masks = mask_ref[...].astype(bf16)
    for b in range(blocks):
        ext_t[FACE + b] = feat_ref[b].T * masks[b:b + 1]
    pl.semaphore_wait(barrier, len(peers))
    halo = [
        send(ext_t.at[pl.ds(FACE, FACE)], halo_in.at[1], ssh.at[0], rsh.at[0], before, x),
        send(ext_t.at[pl.ds(blocks, FACE)], halo_in.at[0], ssh.at[1], rsh.at[1], after, x),
    ]

    perm = (
        lax.broadcasted_iota(jnp.int32, (voxels, voxels), 0) == child_order((voxels, voxels))
    ).astype(bf16)
    map_p[...] = dot(map_ref[...].astype(bf16), perm)
    keep = dot(masks, perm)
    row_ids = lax.broadcasted_iota(jnp.int32, (voxels, voxels), 0).astype(f32)

    def transpose_weight(k, c):
        weight = ws_ref[k].T
        ws_k[k] = weight
        ws_t[:, pl.ds(pl.multiple_of(k * channels, channels), channels)] = weight
        return c

    def gather(some, weights):
        def body(k, c):
            if weights:
                transpose_weight(k, c)
            maps = map_p[pl.ds(pl.multiple_of(k * blocks, blocks), blocks), :]
            for b in some:
                row = maps[b:b + 1] - table_ref[blocks + b, k].astype(f32)
                tile_bk = (row_ids == row).astype(bf16)
                picks[k, :, lanes(b)] = tile_bk
                gathered[k, :, lanes(b)] = dot(ext_t[table_ref[b, k]], tile_bk).astype(bf16)
            return c
        lax.fori_loop(0, offsets, body, 0, unroll=9)

    gather(range(FACE, blocks - FACE), True)
    for copy in halo:
        copy.wait_recv()
    for i in range(FACE):
        ext_t[i] = halo_in[0, i]
        ext_t[FACE + blocks + i] = halo_in[1, i]
    gather(list(range(FACE)) + list(range(blocks - FACE, blocks)), False)

    flat_g = gathered.reshape(offsets * channels, wide)
    flat_p = picks.reshape(offsets * voxels, wide)
    for p in range(blocks // 2):
        cols = pl.ds(p * 2 * voxels, 2 * voxels)
        pre_t[:, cols] = dot(ws_t[...], flat_g[:, cols])
    for b in range(blocks):
        pre = pre_t[:, lanes(b)]
        sig = jax.nn.sigmoid(pre)
        keep_b = keep[b:b + 1]
        hid = (keep_b * (pre * sig)).T.astype(bf16)
        for c in range(8):
            hidden[b * 16:(b + 1) * 16, c * channels:(c + 1) * channels] = hid[c * 16:(c + 1) * 16]
        factor[lanes(b), :] = (keep_b * sig * (1.0 + pre * (1.0 - sig))).T

    lane = lax.broadcasted_iota(jnp.int32, (1, voxels), 1)
    spot = lane % 16
    target = 16 * (spot // 4) + 4 * ((spot // 2) % 2) + spot % 2
    for b in range(blocks):
        target = target + jnp.where(lane // 16 == b, table_ref[2 * blocks, b], 0)
    scatter = (
        lax.broadcasted_iota(jnp.int32, (cot_ref.shape[0], voxels), 0) == target
    ).astype(bf16)
    picked = dot(scatter, cot_ref[...], ((0,), (0,))).astype(bf16)
    dchildren = dot(picked, wd_ref[...], ((1,), (1,)))
    grad_down[...] = dot(hidden[...], picked, ((0,), (0,)))
    pairs[...] = jnp.zeros_like(pairs)
    for b in range(blocks):
        for c in range(8):
            rows = slice(b * voxels + c * 16, b * voxels + (c + 1) * 16)
            part = dchildren[b * 16:(b + 1) * 16, c * channels:(c + 1) * channels]
            dpre[rows, :] = (part * factor[rows, :]).astype(bf16)
        half = (b % 2) * voxels
        pairs[b // 2, half:half + voxels, half:half + voxels] = dpre[lanes(b), :]

    def weight_grad(j, c):
        rows = pl.ds(pl.multiple_of(j * 3 * channels, channels), 3 * channels)
        grad_sub[rows, :] = dot(flat_g[rows, :], dpre[...])
        return c

    lax.fori_loop(0, offsets // 3, weight_grad, 0, unroll=3)

    chip_rows = offsets * channels // (ny * nz)
    own = chip_rows // 2

    full = HALF_T * TILE_ROWS

    def stage_first(yy, c):
        first = pl.multiple_of(yy * nz * chip_rows, 16)
        slab = grad_sub[pl.ds(first, nz * chip_rows), :]
        for zz in range(nz):
            for cc in range(2):
                start = (zz * 2 + cc) * own
                parts[cc, 0, yy, zz] = slab[start:start + full]
        send0[0, yy] = parts[other, 0, yy].astype(bf16)
        return c

    def stage_second(yy, c):
        first = pl.multiple_of(yy * nz * chip_rows, 16)
        slab = grad_sub[pl.ds(first, nz * chip_rows), :]
        down = grad_down[pl.ds(pl.multiple_of(yy * channels, channels), channels), :]
        for zz in range(nz):
            for cc in range(2):
                start = (zz * 2 + cc) * own
                parts[cc, 1, zz, yy, 0:TILE_ROWS, :] = jnp.concatenate(
                    [slab[start + full:start + own], jnp.zeros((TILE_ROWS - own + full, channels), f32)],
                    axis=0,
                )
                start = (zz * 2 + cc) * TILE_ROWS
                for i in range(2):
                    rows = slice((i + 1) * TILE_ROWS, (i + 2) * TILE_ROWS)
                    parts[cc, 1, zz, yy, rows, :] = down[
                        start:start + TILE_ROWS, i * 128:(i + 1) * 128
                    ]
        return c

    def cast_second(i, c):
        send0[1, i] = parts[other, 1, i].astype(bf16)
        return c

    def send_half(h):
        return send(send0.at[h], recv0.at[h], ss0.at[h], rs0.at[h], place(y, z, other), x)

    lax.fori_loop(0, ny, stage_first, 0)
    step0 = [send_half(0)]
    lax.fori_loop(0, ny, stage_second, 0)
    lax.fori_loop(0, nz, cast_second, 0)
    step0.append(send_half(1))

    def spread(j, c):
        rows = pl.ds(pl.multiple_of(j * 3 * voxels, voxels), 3 * voxels)
        for p in range(blocks // 2):
            cols = pl.ds(p * 2 * voxels, 2 * voxels)
            both = dot(flat_p[rows, cols], pairs[p]).astype(bf16)
            for q in range(3):
                for i in range(2):
                    spread_v[(j * 3 + q) * blocks + 2 * p + i] = both[
                        q * voxels:(q + 1) * voxels, i * channels:(i + 1) * channels
                    ]
        return c

    early = offsets // 9
    lax.fori_loop(0, early, spread, 0)

    step1 = []
    for h in range(2):
        step0[h].wait_recv()

        def add_core(i, c, h=h):
            total = parts[core, h, i] + recv0[h, i].astype(f32)
            acc1[h, i] = total
            send1[h, i] = total.astype(bf16)
            return c

        lax.fori_loop(0, ny, add_core, 0)
        for d in range(ny - 1):
            to = y_peers[d] if h == 0 else z_peers[d]
            t = place(to, z, core) if h == 0 else place(y, to, core)
            step1.append(send(send1.at[h, to], recv1.at[h, d], ss1.at[h, d], rs1.at[h, d], t, x))

    sort_v[...] = jnp.zeros_like(sort_v)
    for i, row in enumerate(sort_rows(erow_ref[...], offsets * blocks)):
        sort_v[i:i + 1, :] = row
    sort_copy = pltpu.make_async_copy(sort_v, sort_s, sort_sem)
    sort_copy.start()
    partial_value = dot(hidden[...], wd_ref[...]).astype(bf16)
    coarse_ref[...] = dot(scatter, partial_value).astype(bf16)
    lax.fori_loop(early, offsets // 3, spread, 0)
    sort_copy.wait()

    def term(i, running):
        running = running * sort_s[2, i].astype(f32)
        running = running + dot(spread_v[sort_s[0, i]], ws_k[sort_s[1, i]])
        seg[i] = running
        return running

    lax.fori_loop(
        0, offsets * blocks, term, jnp.zeros((voxels, channels), f32), unroll=8
    )

    def block_grad(e):
        return seg[sort_s[3, e]] * sort_s[4, e].astype(f32)

    for i in range(FACE):
        out_h[0, i] = block_grad(i).astype(bf16)
        out_h[1, i] = block_grad(FACE + blocks + i).astype(bf16)
    returns = [
        send(out_h.at[0], in_h.at[1], ssg.at[0], rsg.at[0], before, x),
        send(out_h.at[1], in_h.at[0], ssg.at[1], rsg.at[1], after, x),
    ]

    step2 = []
    for h in range(2):
        for copy in step1[h * (ny - 1):(h + 1) * (ny - 1)]:
            copy.wait_recv()
        mine = y if h == 0 else z

        def add_axis(i, c, h=h, mine=mine):
            total = acc1[h, mine, i]
            for d in range(ny - 1):
                total = total + recv1[h, d, i].astype(f32)
            acc2[h, i] = total
            return c

        lax.fori_loop(0, nz, add_axis, 0)
        for d in range(nz - 1):
            to = z_peers[d] if h == 0 else y_peers[d]
            t = place(y, to, core) if h == 0 else place(to, z, core)
            step2.append(send(acc2.at[h, to], recv2.at[h, d], ss2.at[h, d], rs2.at[h, d], t, x))

    for copy in returns:
        copy.wait_recv()
    keep_u = mask_ref[...].astype(f32)
    for b in range(blocks):
        total = block_grad(FACE + b)
        if b < FACE:
            total = total + in_h[0, b].astype(f32)
        if b >= blocks - FACE:
            total = total + in_h[1, b - (blocks - FACE)].astype(f32)
        column = jnp.broadcast_to(keep_u[b:b + 1], total.shape).T
        grad_ref[b] = (column * total).astype(bf16)

    for h in range(2):
        for copy in step2[h * (nz - 1):(h + 1) * (nz - 1)]:
            copy.wait_recv()
        total = acc2[h, z if h == 0 else y]
        for d in range(nz - 1):
            total = total + recv2[h, d]
        share[h] = total
    recv3[x] = share[...]
    step3 = [
        send(share, recv3.at[x], ss3.at[d], rs3.at[d], tile, xx) for d, xx in enumerate(x_peers)
    ]
    for copy in step3:
        copy.wait_recv()
    total = recv3[0]
    for i in range(1, nx):
        total = total + recv3[i]
    total = total * scale
    half = HALF_T * TILE_ROWS
    sub_ref[0:half, :] = total[0]
    sub_ref[half:own, :] = total[1, 0:own - half]
    for i in range(2):
        down_ref[pl.ds(i, TILE_ROWS, 2), :] = total[1, (i + 1) * TILE_ROWS:(i + 2) * TILE_ROWS]
    for copy in copies:
        copy.wait_send()


def finish_kernel(*refs):
    arrays = len(refs) // 2
    for source, result in zip(refs[:arrays], refs[arrays:]):
        result[...] = source[...]


def finish(*arrays):
    vmem = pl.BlockSpec(memory_space=pltpu.VMEM)
    return pl.pallas_call(
        finish_kernel,
        out_shape=tuple(jax.ShapeDtypeStruct(a.shape, a.dtype) for a in arrays),
        in_specs=[vmem] * len(arrays),
        out_specs=(vmem,) * len(arrays),
    )(*arrays)


def on_device(
    features,
    w_sub,
    w_down,
    cotangent,
    vox_mask,
    nbr_owner,
    nbr_slot,
    voxel_map,
    parent_slot,
    parent_octant,
):
    _, blocks, voxels, channels = features.shape
    offsets = w_sub.shape[0]
    coarse_channels = w_down.shape[2]
    nx, tiles = lax.axis_size("dp"), lax.axis_size("tile")
    ny = 8
    nz = tiles // (2 * ny)
    f32, bf16, i32 = jnp.float32, jnp.bfloat16, jnp.int32
    tile_index = lax.axis_index("tile")
    owner, slot = nbr_owner[0], nbr_slot[0]
    present = owner >= 0
    position = jnp.where(present, (owner - tile_index) * blocks + FACE + slot, 0)
    octant = parent_octant[0]
    corner = (
        parent_slot[0] * voxels + 64 * (octant // 4) + 8 * ((octant // 2) % 2) + 2 * (octant % 2)
    )
    table = jnp.concatenate([
        position,
        jnp.where(present, 0, NO_VOXEL),
        jnp.pad(corner, (0, offsets - blocks))[None],
    ])
    maps = jnp.transpose(voxel_map[0], (1, 0, 2)).reshape(-1, voxels)
    entry = jnp.pad(
        position.T.reshape(1, -1), ((0, 0), (0, 256 - offsets * blocks)),
        constant_values=NO_BLOCK,
    )
    scale = float(nx * tiles * blocks * voxels) ** (-0.5)
    wide = blocks * voxels
    ext = blocks + 2 * FACE
    rows = HALF_T * TILE_ROWS
    own_rows = offsets * channels // tiles
    vmem = pl.BlockSpec(memory_space=pltpu.VMEM)
    smem = pl.BlockSpec(memory_space=pltpu.SMEM)
    dma = pltpu.SemaphoreType.DMA
    coarse_rows = cotangent.shape[1] * cotangent.shape[2]
    coarse, grad, sub, down = pl.pallas_call(
        functools.partial(kernel, (nx, ny, nz), scale),
        out_shape=(
            jax.ShapeDtypeStruct((coarse_rows, coarse_channels), bf16),
            jax.ShapeDtypeStruct((blocks, voxels, channels), bf16),
            jax.ShapeDtypeStruct((own_rows, channels), f32),
            jax.ShapeDtypeStruct((2 * TILE_ROWS, channels), f32),
        ),
        in_specs=[smem] + [vmem] * 7,
        out_specs=(vmem,) * 4,
        scratch_shapes=[
            pltpu.VMEM((offsets, voxels, wide), bf16),
            pltpu.VMEM((offsets, channels, wide), bf16),
            pltpu.VMEM((ext, channels, voxels), bf16),
            pltpu.VMEM((2, FACE, channels, voxels), bf16),
            pltpu.VMEM((channels, offsets * channels), bf16),
            pltpu.VMEM((offsets, channels, channels), bf16),
            pltpu.VMEM((offsets * blocks, voxels, channels), bf16),
            pltpu.VMEM((offsets * blocks, voxels), f32),
            pltpu.VMEM((channels, wide), f32),
            pltpu.VMEM((wide // 8, 8 * channels), bf16),
            pltpu.VMEM((wide, channels), f32),
            pltpu.VMEM((wide, channels), bf16),
            pltpu.VMEM((blocks // 2, 2 * voxels, 2 * channels), bf16),
            pltpu.VMEM((offsets * channels, channels), f32),
            pltpu.VMEM((8 * channels, coarse_channels), f32),
            pltpu.VMEM((TILE_ROWS, 256), i32),
            pltpu.SMEM((TILE_ROWS, 256), i32),
            pltpu.VMEM((offsets * blocks, voxels, channels), f32),
            pltpu.VMEM((2, 2, ny, nz, rows, 128), f32),
            pltpu.VMEM((2, ny, nz, rows, 128), bf16),
            pltpu.VMEM((2, ny, nz, rows, 128), bf16),
            pltpu.VMEM((2, ny, nz, rows, 128), f32),
            pltpu.VMEM((2, ny, nz, rows, 128), bf16),
            pltpu.VMEM((2, ny - 1, nz, rows, 128), bf16),
            pltpu.VMEM((2, nz, rows, 128), f32),
            pltpu.VMEM((2, nz - 1, rows, 128), f32),
            pltpu.VMEM((nx, 2, rows, 128), f32),
            pltpu.VMEM((2, rows, 128), f32),
            pltpu.VMEM((2, FACE, voxels, channels), bf16),
            pltpu.VMEM((2, FACE, voxels, channels), bf16),
            dma,
            dma((2,)), dma((2,)),
            dma((2, ny - 1)), dma((2, ny - 1)),
            dma((2, nz - 1)), dma((2, nz - 1)),
            dma((nx - 1,)), dma((nx - 1,)),
            dma((2,)), dma((2,)),
            dma((2,)), dma((2,)),
        ],
        compiler_params=pltpu.CompilerParams(
            collective_id=0, has_side_effects=True, vmem_limit_bytes=60 * 1024 * 1024
        ),
    )(
        table, entry, features[0], maps, w_sub,
        w_down.reshape(-1, coarse_channels), cotangent[0].reshape(-1, coarse_channels),
        vox_mask[0],
    )
    coarse, grad, sub, down = finish(coarse, grad, sub, down)
    return (
        coarse.reshape(cotangent.shape), grad[None], sub.reshape(-1), down.reshape(-1),
    )


def solution(mesh):
    in_specs = (
        P("dp", "tile", None, None),
        P(),
        P(),
        P("dp", "tile", None, None),
        P("dp", "tile", None),
        P("dp", "tile", None),
        P("dp", "tile", None),
        P("dp", "tile", None, None),
        P("dp", "tile"),
        P("dp", "tile"),
    )
    out_specs = (P("dp", "tile", None, None), P("dp", "tile", None, None), P("tile"), P("tile"))
    return jax.shard_map(
        on_device, mesh=mesh, in_specs=in_specs, out_specs=out_specs, check_vma=False
    )
```
